256 devices in a mesh: kx: 8 (over x_lo, y), kz: 32 (over z, x_hi, core).
Axes of the slice: x: 4 (x_hi: 2, x_lo: 2; x = x_hi * 2 + x_lo), y: 4, z: 8, core: 2. Of those that a mesh axis runs over, the one named last changes fastest.
Arguments:
- forcing: float32 [1536, 4, 128, 256], P(('kx', 'kz')), may hold values from -20 to 20
- kx_wave: int32 [128], P('kx'), may hold values from 0 to 64
- kz_wave: int32 [256], P('kz'), may hold values from -32 to 32
Outputs:
- fields: float32 [1536, 4, 128, 256], P(('kx', 'kz'))
The draws below stay inside these ranges and needn't reach their ends.
All inputs are finite; a program needn't handle non-finite values.
Results may differ from the reference program's by a relative error of at most 0.00007.
Values sent between devices are 32-bit elements; how exact they have to be, the bound alone decides.
No kernel may reach another device: no remote copies, remote signals or barrier semaphores. Data moves between devices by JAX's collectives and lax.ppermute only.
A program may use at most 192 MiB of HBM per device.

```python
import jax
import jax.numpy as jnp
from jax import lax

NY = 1536
MX = 128
MZ = 256


def draw_forcing(key, part):
    key = jax.random.fold_in(key, 7)
    key_coef, key_noise = jax.random.split(key)
    points = (jnp.arange(NY, dtype=jnp.float32) + 1.0) / jnp.float32(NY + 1)
    orders = jnp.arange(4, dtype=jnp.float32) + 1.0
    profiles = jnp.sin(jnp.float32(jnp.pi) * orders[:, None] * points[None, :])
    weights = 0.7 * jnp.clip(jax.random.normal(key_coef, (4, 4, MX, MZ), jnp.float32), -3.0, 3.0)
    noise = 1.5 * jnp.clip(jax.random.normal(key_noise, (NY, 4, MX, MZ), jnp.float32), -4.0, 4.0)
    smooth = profiles[0][:, None, None, None] * weights[0]
    smooth = smooth + profiles[1][:, None, None, None] * weights[1]
    smooth = smooth + profiles[2][:, None, None, None] * weights[2]
    smooth = smooth + profiles[3][:, None, None, None] * weights[3]
    return (smooth + noise).astype(jnp.float32)


def with_ends(values, own_key, low, largest):
    place = [jax.random.randint(jax.random.fold_in(own_key, axis), (), 0, length) for axis, length in enumerate(values.shape)]
    main_axis = values.shape.index(max(values.shape))
    neighbour = place[:main_axis] + [(place[main_axis] + 1) % values.shape[main_axis]] + place[main_axis + 1:]
    return values.at[tuple(place)].set(low).at[tuple(neighbour)].set(largest)


def setup_inputs(seed: int = 0) -> dict:
    seeds = jax.random.split(jax.random.key(seed), 4)
    forcing = draw_forcing(jax.random.fold_in(seeds[3], 71), 0)
    kx_wave = with_ends(jax.random.randint(seeds[1], (MX,), 0, MX // 2 + 1), jax.random.fold_in(seeds[1], 1), 0, (MX // 2 + 1) - 1).astype(jnp.int32)
    kz_wave = with_ends(jax.random.randint(seeds[2], (MZ,), -(MZ // 8), MZ // 8 + 1), jax.random.fold_in(seeds[2], 1), -(MZ // 8), (MZ // 8 + 1) - 1).astype(jnp.int32)
    return dict(forcing=forcing, kx_wave=kx_wave, kz_wave=kz_wave)


implicit_shift = 4000.0
alpha_x = 0.25
beta_z = 2.0 / 3.0

def tables(count):
    indices = jnp.arange(count, dtype=jnp.int32) + 1
    products = indices[:, None] * indices[None, :] % (2 * (count + 1))
    scale_term = jnp.sqrt(jnp.float32(2.0) / jnp.float32(count + 1))
    eigen_basis = scale_term * jnp.sin(jnp.float32(jnp.pi) * products.astype(jnp.float32) / jnp.float32(count + 1))
    angles = jnp.float32(jnp.pi) * indices.astype(jnp.float32) / jnp.float32(2 * (count + 1))
    eigen_values = -jnp.float32((count + 1) ** 2) * jnp.sin(angles) ** 2
    return (eigen_basis, eigen_values)

def helmholtz(columns, wave_sq, eigen_basis, eigen_values, count):
    upper_limit = lax.Precision.HIGHEST
    shifted = wave_sq + implicit_shift
    width = columns.shape[2]
    coeffs = jnp.dot(eigen_basis, columns.reshape(count, -1), precision=upper_limit).reshape(count, 4, width)
    phi_inverse_operator = 1.0 / (eigen_values[:, None] - shifted[None, :])
    velocity_inverse_operator = 1.0 / (eigen_values[:, None] - wave_sq[None, :])
    c_omega = -implicit_shift * coeffs[:, 2:4] * phi_inverse_operator[:, None]
    phi_coefficient = -implicit_shift * coeffs[:, 0:2] * phi_inverse_operator[:, None]
    c_v = phi_coefficient * velocity_inverse_operator[:, None]
    boundary_rows = jnp.stack([4.0 * eigen_basis[0] - eigen_basis[1], 4.0 * eigen_basis[count - 1] - eigen_basis[count - 2]])
    wall_v = jnp.dot(boundary_rows, c_v.reshape(count, -1), precision=upper_limit).reshape(2, 2, width)
    inv_step_sq = jnp.float32((count + 1) ** 2) / 4.0
    source_terms = -inv_step_sq * jnp.stack([eigen_basis[0], eigen_basis[count - 1]], axis=1)
    homogeneous_phi_profile = source_terms[:, :, None] * phi_inverse_operator[:, None, :]
    homogeneous_velocity_profile = homogeneous_phi_profile * velocity_inverse_operator[:, None, :]
    influence_matrix = jnp.einsum('vo,ocy->vcy', boundary_rows, homogeneous_velocity_profile, precision=upper_limit)
    determinant = influence_matrix[0, 0] * influence_matrix[1, 1] - influence_matrix[0, 1] * influence_matrix[1, 0]
    lower_amplitude = -(influence_matrix[1, 1] * wall_v[0] - influence_matrix[0, 1] * wall_v[1]) / determinant
    upper_amplitude = -(influence_matrix[0, 0] * wall_v[1] - influence_matrix[1, 0] * wall_v[0]) / determinant
    phi_coefficient = phi_coefficient + lower_amplitude[None] * homogeneous_phi_profile[:, 0:1] + upper_amplitude[None] * homogeneous_phi_profile[:, 1:2]
    joined = jnp.concatenate([phi_coefficient, c_omega], axis=1).reshape(count, -1)
    return jnp.dot(eigen_basis, joined, precision=upper_limit).reshape(count, 4, width)

def reference(forcing, kx_wave, kz_wave):
    eigen_basis, eigen_values = tables(NY)
    wave_sq = (alpha_x * kx_wave.astype(jnp.float32))[:, None] ** 2 + (beta_z * kz_wave.astype(jnp.float32))[None, :] ** 2
    moved = jnp.moveaxis(forcing, 2, 0)

    def one_slice(pair):
        return helmholtz(pair[0], pair[1], eigen_basis, eigen_values, NY)
    solved = lax.map(one_slice, (moved, wave_sq))
    return jnp.moveaxis(solved, 0, 2)
```

```python
import functools
import math

import jax
import jax.numpy as jnp
from jax import lax
from jax.experimental import pallas as pl
from jax.experimental.pallas import tpu as pltpu
from jax.sharding import PartitionSpec as P

NY = 1536
N = NY + 1
H2 = (2.0 / N) ** 2
SHIFT = 4000.0
KAPPA = SHIFT * H2
ALPHA_X = 0.25
BETA_Z = 2.0 / 3.0
PTS = 6
BLK = 12
GRP = 16
F32 = jnp.float32


def chain(eps, n):
    p = [None, jnp.ones_like(eps)]
    diff = 1.0 + eps
    for _ in range(2, n + 1):
        p.append(p[-1] + diff)
        diff = diff + eps * p[-1]
    return p


def angle(eps):
    x2 = 0.25 * eps
    series = 1.0 + x2 * (-1.0 / 6.0 + x2 * (3.0 / 40.0 + x2 * (-15.0 / 336.0 + x2 * (105.0 / 3456.0))))
    return jnp.sqrt(eps) * series


def moments_kernel(s_ref, w_ref, x_ref, r_ref, up_ref, mid_ref, q_ref, qo_ref):
    core = s_ref[0]
    turn = s_ref[3]
    step = pl.program_id(0)
    lane = lax.broadcasted_iota(jnp.int32, (8, 128), 1) // 8
    sub = lax.broadcasted_iota(jnp.int32, (8, 128), 0)

    def kz_row(half):
        acc = [jnp.zeros((8, 128), F32), jnp.zeros((8, 128), F32)]
        for j in range(32):
            place = lax.rem(j // 4 + turn, 8) + 8 * (j % 4) - GRP * half
            acc[j % 2] = acc[j % 2] + jnp.where(lane == place, w_ref[j], 0.0)
        row = acc[0][4:5, :] + acc[1][0:1, :]
        return jnp.broadcast_to(row, (8, 128))

    kz_own = (BETA_Z * kz_row(core)) ** 2
    kz_oth = (BETA_Z * kz_row(1 - core)) ** 2
    tiles = up_ref.shape[0]

    def tile(first, second):
        for i in range(tiles):
            at = 2 * (step * tiles + i)
            kx = (ALPHA_X * jnp.where(sub < 4, w_ref[at], w_ref[at + 1])) ** 2
            rows = pl.ds(8 * i, 8)
            q = kx + kz_own
            q_ref[rows, :] = q
            qo_ref[rows, :] = kx + kz_oth
            ps = chain(H2 * (q + SHIFT), BLK)
            pq = chain(H2 * q, BLK)
            for c in range(4):
                f = [first[m, c, rows, :] for m in range(PTS)] + [second[m, c, rows, :] for m in range(PTS)]
                own = ps[BLK] * f[0]
                nxt = ps[1] * f[1]
                mid = ps[1] * f[1]
                for m in range(1, BLK):
                    own = own + ps[BLK - m] * f[m]
                for m in range(2, BLK):
                    nxt = nxt + ps[m] * f[m]
                    mid = mid + ps[min(m, BLK - m)] * f[m]
                up_ref[i, c] = KAPPA * own
                up_ref[i, 4 + c] = KAPPA * nxt
                mid_ref[i, c] = KAPPA * mid
                if c < 2:
                    own = pq[BLK] * f[0]
                    nxt = pq[1] * f[1]
                    for m in range(1, BLK):
                        own = own + pq[BLK - m] * f[m]
                    for m in range(2, BLK):
                        nxt = nxt + pq[m] * f[m]
                    up_ref[i, 8 + c] = KAPPA * own
                    up_ref[i, 10 + c] = KAPPA * nxt

    @pl.when(core == 0)
    def _():
        tile(x_ref, r_ref)

    @pl.when(core != 0)
    def _():
        tile(r_ref, x_ref)


def sources(m_ref, own, nxt):
    return (
        [m_ref[0, own]]
        + [m_ref[d, own] + m_ref[d - 1, nxt] for d in range(1, GRP)]
        + [m_ref[GRP - 1, nxt]]
    )


def group_kernel(s_ref, m_ref, q_ref, o_ref):
    group = s_ref[1]
    q = q_ref[...]
    rho = jnp.exp(-BLK * angle(H2 * (q + SHIFT)))
    res = [None] * 12
    for c in range(4):
        t = sources(m_ref, c, 4 + c)
        right = t[0]
        for d in range(1, GRP + 1):
            right = rho * right + t[d]
        left = t[GRP]
        for d in range(GRP - 1, -1, -1):
            left = rho * left + t[d]
        res[c] = right
        res[4 + c] = left
    tq = angle(H2 * q)
    end = jnp.exp(-N * tq)
    inv = 1.0 / jnp.where(q > 0.0, 1.0 - end * end, 1.0)
    sq = [sources(m_ref, 8 + c, 10 + c) for c in range(2)]
    for c in range(2):
        res[8 + c] = jnp.zeros_like(q)
        res[10 + c] = jnp.zeros_like(q)
    for d in range(GRP + 1):
        place = (BLK * (GRP * group + d) + 1).astype(F32)
        fall = jnp.exp(-place * tq)
        rise = (jnp.exp((place - N) * tq) - end * fall) * inv
        rise = jnp.where(q > 0.0, rise, place * (1.0 / N))
        fall = fall - end * rise
        for c in range(2):
            res[8 + c] = res[8 + c] + fall * sq[c][d]
            res[10 + c] = res[10 + c] + rise * sq[c][d]
    for k in range(o_ref.shape[0]):
        for n in range(12):
            o_ref[k, n] = res[n]


def solve_kernel(s_ref, m_ref, g_ref, q_ref, o_ref):
    group = s_ref[1]
    groups = g_ref.shape[0]
    q = q_ref[...]
    es = H2 * (q + SHIFT)
    eq = H2 * q
    ts = angle(es)
    tq = angle(eq)
    rho = jnp.exp(-BLK * ts)
    rho_g = jnp.exp(-(BLK * GRP) * ts)
    sinh_s = jnp.sqrt(es * (1.0 + 0.25 * es))
    sinh_q = jnp.sqrt(eq * (1.0 + 0.25 * eq))
    scale = 0.5 / (sinh_s * chain(es, BLK)[BLK])
    end_s = jnp.exp(-N * ts)
    inv_s = 1.0 / (1.0 - end_s * end_s)
    end_q = jnp.exp(-N * tq)
    positive = q > 0.0
    inv_q = 1.0 / jnp.where(positive, 1.0 - end_q * end_q, 1.0)
    coth_s = sinh_s * (1.0 + end_s * end_s) * inv_s
    csch_s = 2.0 * sinh_s * end_s * inv_s
    coth_q = jnp.where(positive, sinh_q * (1.0 + end_q * end_q) * inv_q, 1.0 / N)
    csch_q = jnp.where(positive, 2.0 * sinh_q * end_q * inv_q, 1.0 / N)
    m_same = (2.0 - es) * coth_s - (2.0 - eq) * coth_q + 0.5 * (es * es - eq * eq)
    m_cross = (2.0 - eq) * csch_q - (2.0 - es) * csch_s
    inv_det = 1.0 / (m_same * m_same - m_cross * m_cross)
    inv_pq = 1.0 / chain(eq, BLK)[BLK]
    gf = group.astype(F32)
    near = jnp.exp(-(gf * (BLK * GRP) + 1.0) * ts)
    far = jnp.exp(-(NY - BLK * GRP - gf * (BLK * GRP)) * ts)
    first = jnp.exp(-ts)
    for c in range(4):
        at_hi = g_ref[0, c]
        from_lo = jnp.zeros_like(q)
        for k in range(groups):
            if k:
                at_hi = rho_g * at_hi + g_ref[k, c]
            from_lo = jnp.where(k < group, rho_g * from_lo + g_ref[k, c], from_lo)
        at_lo = g_ref[groups - 1, 4 + c]
        from_hi = jnp.zeros_like(q)
        for k in range(groups - 1, -1, -1):
            if k < groups - 1:
                at_lo = rho_g * at_lo + g_ref[k, 4 + c]
            from_hi = jnp.where(k > group, rho_g * from_hi + g_ref[k, 4 + c], from_hi)
        x_lo = scale * first * at_lo
        x_hi = scale * at_hi
        if c < 2:
            y_lo = g_ref[0, 8 + c]
            y_hi = g_ref[0, 10 + c]
            for k in range(1, groups):
                y_lo = y_lo + g_ref[k, 8 + c]
                y_hi = y_hi + g_ref[k, 10 + c]
            alpha = (end_s * x_hi - x_lo) * inv_s
            beta = (end_s * x_lo - x_hi) * inv_s
            phi_lo = 2.0 * sinh_s * (x_lo + end_s * beta)
            phi_hi = 2.0 * sinh_s * (x_hi + end_s * alpha)
            w_lo = (2.0 - es) * phi_lo - (2.0 - eq) * (y_lo * inv_pq)
            w_hi = (2.0 - es) * phi_hi - (2.0 - eq) * (y_hi * inv_pq)
            wall_lo = (m_same * w_lo - m_cross * w_hi) * inv_det - x_lo
            wall_hi = (m_same * w_hi - m_cross * w_lo) * inv_det - x_hi
        else:
            wall_lo = -x_lo
            wall_hi = -x_hi
        alpha = (wall_lo - end_s * wall_hi) * inv_s
        beta = (wall_hi - end_s * wall_lo) * inv_s
        t = [scale * v for v in sources(m_ref, c, 4 + c)]
        back = scale * from_hi + beta * far
        falls = [None] * (GRP + 1)
        falls[GRP] = back
        for d in range(GRP - 1, -1, -1):
            back = rho * (back + t[d + 1])
            falls[d] = back
        ahead = scale * from_lo + alpha * near + t[0]
        for d in range(GRP + 1):
            if d:
                ahead = rho * ahead + t[d]
            value = ahead + falls[d]
            if d < GRP:
                o_ref[d, c] = value
            if d:
                o_ref[d - 1, 4 + c] = value


def middle_kernel(s_ref, b_ref, mid_ref, q_ref, own_ref, send_ref):
    core = s_ref[0]

    def tile(lower, upper):
        for i in range(b_ref.shape[0]):
            ps = chain(H2 * (q_ref[pl.ds(8 * i, 8), :] + SHIFT), BLK)
            ratio = ps[PTS] / ps[BLK]
            for c in range(4):
                a = b_ref[i, c]
                b = b_ref[i, 4 + c]
                x = ratio * (a + b + mid_ref[i, c])
                lower[i, c] = a
                lower[i, 4 + c] = x
                upper[i, c] = x
                upper[i, 4 + c] = b

    @pl.when(core == 0)
    def _():
        tile(own_ref, send_ref)

    @pl.when(core != 0)
    def _():
        tile(send_ref, own_ref)


def points_kernel(s_ref, x_ref, own_ref, r_ref, q_ref, qo_ref, o_ref):
    core = s_ref[0]

    def tile(half, ends, waves):
        lanes = pl.ds(128 * half, 128)
        for i in range(ends.shape[0]):
            rows = pl.ds(8 * i, 8)
            ps = chain(H2 * (waves[rows, :] + SHIFT), PTS)
            ratio = [None] + [ps[m] / ps[m + 1] for m in range(1, PTS)]
            for c in range(4):
                a = ends[i, c]
                y = [None, KAPPA * x_ref[1, c, rows, lanes] + a]
                for m in range(2, PTS):
                    y.append(KAPPA * x_ref[m, c, rows, lanes] + ratio[m - 1] * y[-1])
                o_ref[0, c, rows, lanes] = a
                value = ends[i, 4 + c]
                for m in range(PTS - 1, 0, -1):
                    value = ratio[m] * (y[m] + value)
                    o_ref[m, c, rows, lanes] = value

    @pl.when(core == 0)
    def _():
        tile(0, own_ref, q_ref)
        tile(1, r_ref, qo_ref)

    @pl.when(core != 0)
    def _():
        tile(0, r_ref, qo_ref)
        tile(1, own_ref, q_ref)


def on_device(forcing, kx_wave, kz_wave):
    ix = lax.axis_index("kx")
    iz = lax.axis_index("kz")
    core = lax.rem(iz, 2)
    chip = iz // 2
    turn = lax.rem(iz - ix + 32, 8)
    place = jnp.stack([core, ix, chip, turn]).astype(jnp.int32)
    both = ("kx", "kz")
    wave_groups = [
        [k * 32 + (k + t) % 8 + 8 * part for k in range(8) for part in range(4)] for t in range(8)
    ]
    core_groups = [[2 * k + c for k in range(GRP)] for c in range(2)]
    pairs = [(i, i ^ 1) for i in range(32)]

    other = lax.dynamic_slice_in_dim(forcing, 128 * (1 - core), 128, axis=3)
    swapped = lax.ppermute(other, "kz", pairs)

    part = iz // 8
    kx8 = lax.dynamic_slice_in_dim(kx_wave, 8 * (part // 2), 8).astype(F32)
    sub = lax.broadcasted_iota(jnp.int32, (8, 128), 0)
    payload = jnp.where(
        sub // 4 == lax.rem(part, 2),
        jnp.broadcast_to(kx8[:, None], (8, 128)),
        jnp.broadcast_to(jnp.tile(kz_wave.astype(F32), 16)[None, :], (8, 128)),
    )
    waves = lax.all_to_all(
        jnp.broadcast_to(payload[None], (32, 8, 128)), both, 0, 0, tiled=True, axis_index_groups=wave_groups
    )

    steps = 4
    tiles = GRP // steps
    rows = 8 * tiles
    tiled = lambda n: pl.BlockSpec((tiles, n, 8, 128), lambda i, s: (i, 0, 0, 0))
    flat = pl.BlockSpec((rows, 128), lambda i, s: (i, 0))
    up, mid, q_own, q_oth = pl.pallas_call(
        moments_kernel,
        grid_spec=pltpu.PrefetchScalarGridSpec(
            num_scalar_prefetch=1,
            grid=(steps,),
            in_specs=[
                pl.BlockSpec((32, 8, 128), lambda i, s: (0, 0, 0)),
                pl.BlockSpec((PTS, 4, rows, 128), lambda i, s: (0, 0, i, s[0])),
                pl.BlockSpec((PTS, 4, rows, 128), lambda i, s: (0, 0, i, 0)),
            ],
            out_specs=[tiled(12), tiled(4), flat, flat],
        ),
        out_shape=[
            jax.ShapeDtypeStruct((GRP, 12, 8, 128), F32),
            jax.ShapeDtypeStruct((GRP, 4, 8, 128), F32),
            jax.ShapeDtypeStruct((128, 128), F32),
            jax.ShapeDtypeStruct((128, 128), F32),
        ],
    )(place, waves, forcing, swapped)

    blocks = lax.all_to_all(up, "kz", 0, 0, tiled=True, axis_index_groups=core_groups)

    whole = lambda *shape: pl.BlockSpec(shape, lambda i, s: (0,) * len(shape))
    my_q = pl.BlockSpec((8, 128), lambda i, s: (s[2], 0))
    message = pl.pallas_call(
        group_kernel,
        grid_spec=pltpu.PrefetchScalarGridSpec(
            num_scalar_prefetch=1,
            grid=(1,),
            in_specs=[whole(GRP, 12, 8, 128), my_q],
            out_specs=whole(8, 12, 8, 128),
        ),
        out_shape=jax.ShapeDtypeStruct((8, 12, 8, 128), F32),
    )(place, blocks, q_own)

    messages = lax.all_to_all(message, "kx", 0, 0, tiled=True)

    ends = pl.pallas_call(
        solve_kernel,
        grid_spec=pltpu.PrefetchScalarGridSpec(
            num_scalar_prefetch=1,
            grid=(1,),
            in_specs=[whole(GRP, 12, 8, 128), whole(8, 12, 8, 128), my_q],
            out_specs=whole(GRP, 8, 8, 128),
        ),
        out_shape=jax.ShapeDtypeStruct((GRP, 8, 8, 128), F32),
    )(place, blocks, messages, q_own)

    ends = lax.all_to_all(ends, "kz", 0, 0, tiled=True, axis_index_groups=core_groups)

    own, send = pl.pallas_call(
        middle_kernel,
        grid_spec=pltpu.PrefetchScalarGridSpec(
            num_scalar_prefetch=1,
            grid=(steps,),
            in_specs=[tiled(8), tiled(4), flat],
            out_specs=[tiled(8), tiled(8)],
        ),
        out_shape=[jax.ShapeDtypeStruct((GRP, 8, 8, 128), F32)] * 2,
    )(place, ends, mid, q_own)

    received = lax.ppermute(send, "kz", pairs)

    return pl.pallas_call(
        points_kernel,
        grid_spec=pltpu.PrefetchScalarGridSpec(
            num_scalar_prefetch=1,
            grid=(steps,),
            in_specs=[
                pl.BlockSpec((PTS, 4, rows, 256), lambda i, s: (0, 0, i, 0)),
                tiled(8),
                tiled(8),
                flat,
                flat,
            ],
            out_specs=pl.BlockSpec((PTS, 4, rows, 256), lambda i, s: (0, 0, i, 0)),
        ),
        out_shape=jax.ShapeDtypeStruct(forcing.shape, F32),
    )(place, forcing, own, received, q_own, q_oth)


def solution(mesh):
    placed = (P(("kx", "kz"), None, None, None), P("kx"), P("kz"))
    return jax.shard_map(
        on_device,
        mesh=mesh,
        in_specs=placed,
        out_specs=P(("kx", "kz"), None, None, None),
        check_vma=False,
    )
```

```python
import jax
import jax.numpy as jnp
from jax import lax
from jax.experimental import pallas as pl
from jax.experimental.pallas import tpu as pltpu
from jax.sharding import PartitionSpec as P

NY = 1536
N = NY + 1
H2 = (2.0 / N) ** 2
SHIFT = 4000.0
KAPPA = SHIFT * H2
ALPHA_X = 0.25
BETA_Z = 2.0 / 3.0
PTS = 6
BLK = 12
GRP = 16
F32 = jnp.float32


def chain(eps, n):
    p = [None, jnp.ones_like(eps)]
    diff = 1.0 + eps
    for _ in range(2, n + 1):
        p.append(p[-1] + diff)
        diff = diff + eps * p[-1]
    return p


def angle(eps):
    x2 = 0.25 * eps
    series = 1.0 + x2 * (-1.0 / 6.0 + x2 * (3.0 / 40.0 + x2 * (-15.0 / 336.0 + x2 * (105.0 / 3456.0))))
    return jnp.sqrt(eps) * series


def moments_kernel(s_ref, w_ref, x_ref, r_ref, up_ref, mid_ref, q_ref, qo_ref):
    core = s_ref[0]
    turn = s_ref[3]
    lane = lax.broadcasted_iota(jnp.int32, (8, 128), 1) // 8
    sub = lax.broadcasted_iota(jnp.int32, (8, 128), 0)

    def kz_row(half):
        acc = [jnp.zeros((8, 128), F32), jnp.zeros((8, 128), F32)]
        for j in range(32):
            place = lax.rem(j // 4 + turn, 8) + 8 * (j % 4) - GRP * half
            acc[j % 2] = acc[j % 2] + jnp.where(lane == place, w_ref[j], 0.0)
        row = acc[0][4:5, :] + acc[1][0:1, :]
        return (BETA_Z * jnp.broadcast_to(row, (8, 128))) ** 2

    kz_own = kz_row(core)
    kz_oth = kz_row(1 - core)

    def tiles(first, second):
        @pl.loop(0, GRP)
        def _(i):
            kx = (ALPHA_X * jnp.where(sub < 4, w_ref[2 * i], w_ref[2 * i + 1])) ** 2
            rows = pl.ds(pl.multiple_of(8 * i, 8), 8)
            q = kx + kz_own
            q_ref[rows, :] = q
            qo_ref[rows, :] = kx + kz_oth
            ps = chain(H2 * (q + SHIFT), BLK)
            pq = chain(H2 * q, BLK)
            for c in range(4):
                f = [first(m, c, rows) for m in range(PTS)] + [second(m, c, rows) for m in range(PTS)]
                own = ps[BLK] * f[0]
                nxt = ps[1] * f[1]
                mid = ps[1] * f[1]
                for m in range(1, BLK):
                    own = own + ps[BLK - m] * f[m]
                for m in range(2, BLK):
                    nxt = nxt + ps[m] * f[m]
                    mid = mid + ps[min(m, BLK - m)] * f[m]
                up_ref[i, c] = KAPPA * own
                up_ref[i, 4 + c] = KAPPA * nxt
                mid_ref[i, c] = KAPPA * mid
                if c < 2:
                    own = pq[BLK] * f[0]
                    nxt = pq[1] * f[1]
                    for m in range(1, BLK):
                        own = own + pq[BLK - m] * f[m]
                    for m in range(2, BLK):
                        nxt = nxt + pq[m] * f[m]
                    up_ref[i, 8 + c] = KAPPA * own
                    up_ref[i, 10 + c] = KAPPA * nxt

    @pl.when(core == 0)
    def _():
        tiles(lambda m, c, rows: x_ref[m, c, rows, :128], lambda m, c, rows: r_ref[m, c, rows, :128])

    @pl.when(core != 0)
    def _():
        tiles(lambda m, c, rows: r_ref[m, c, rows, 128:], lambda m, c, rows: x_ref[m, c, rows, 128:])


def sources(m_ref, own, nxt):
    return (
        [m_ref[0, own]]
        + [m_ref[d, own] + m_ref[d - 1, nxt] for d in range(1, GRP)]
        + [m_ref[GRP - 1, nxt]]
    )


def group_kernel(s_ref, m_ref, q_ref, o_ref):
    group = s_ref[1]
    q = q_ref[pl.ds(pl.multiple_of(8 * s_ref[2], 8), 8), :]
    rho = jnp.exp(-BLK * angle(H2 * (q + SHIFT)))
    res = [None] * 12
    for c in range(4):
        t = sources(m_ref, c, 4 + c)
        right = t[0]
        for d in range(1, GRP + 1):
            right = rho * right + t[d]
        left = t[GRP]
        for d in range(GRP - 1, -1, -1):
            left = rho * left + t[d]
        res[c] = right
        res[4 + c] = left
    tq = angle(H2 * q)
    end = jnp.exp(-N * tq)
    inv = 1.0 / jnp.where(q > 0.0, 1.0 - end * end, 1.0)
    sq = [sources(m_ref, 8 + c, 10 + c) for c in range(2)]
    for c in range(2):
        res[8 + c] = jnp.zeros_like(q)
        res[10 + c] = jnp.zeros_like(q)
    for d in range(GRP + 1):
        place = (BLK * (GRP * group + d) + 1).astype(F32)
        fall = jnp.exp(-place * tq)
        rise = (jnp.exp((place - N) * tq) - end * fall) * inv
        rise = jnp.where(q > 0.0, rise, place * (1.0 / N))
        fall = fall - end * rise
        for c in range(2):
            res[8 + c] = res[8 + c] + fall * sq[c][d]
            res[10 + c] = res[10 + c] + rise * sq[c][d]
    for k in range(o_ref.shape[0]):
        for n in range(12):
            o_ref[k, n] = res[n]


def solve_kernel(s_ref, m_ref, g_ref, q_ref, o_ref):
    group = s_ref[1]
    groups = g_ref.shape[0]
    q = q_ref[pl.ds(pl.multiple_of(8 * s_ref[2], 8), 8), :]
    es = H2 * (q + SHIFT)
    eq = H2 * q
    ts = angle(es)
    tq = angle(eq)
    rho = jnp.exp(-BLK * ts)
    rho_g = jnp.exp(-(BLK * GRP) * ts)
    sinh_s = jnp.sqrt(es * (1.0 + 0.25 * es))
    sinh_q = jnp.sqrt(eq * (1.0 + 0.25 * eq))
    scale = 0.5 / (sinh_s * chain(es, BLK)[BLK])
    end_s = jnp.exp(-N * ts)
    inv_s = 1.0 / (1.0 - end_s * end_s)
    end_q = jnp.exp(-N * tq)
    positive = q > 0.0
    inv_q = 1.0 / jnp.where(positive, 1.0 - end_q * end_q, 1.0)
    coth_s = sinh_s * (1.0 + end_s * end_s) * inv_s
    csch_s = 2.0 * sinh_s * end_s * inv_s
    coth_q = jnp.where(positive, sinh_q * (1.0 + end_q * end_q) * inv_q, 1.0 / N)
    csch_q = jnp.where(positive, 2.0 * sinh_q * end_q * inv_q, 1.0 / N)
    m_same = (2.0 - es) * coth_s - (2.0 - eq) * coth_q + 0.5 * (es * es - eq * eq)
    m_cross = (2.0 - eq) * csch_q - (2.0 - es) * csch_s
    inv_det = 1.0 / (m_same * m_same - m_cross * m_cross)
    inv_pq = 1.0 / chain(eq, BLK)[BLK]
    gf = group.astype(F32)
    near = jnp.exp(-(gf * (BLK * GRP) + 1.0) * ts)
    far = jnp.exp(-(NY - BLK * GRP - gf * (BLK * GRP)) * ts)
    first = jnp.exp(-ts)
    for c in range(4):
        at_hi = g_ref[0, c]
        from_lo = jnp.zeros_like(q)
        for k in range(groups):
            if k:
                at_hi = rho_g * at_hi + g_ref[k, c]
            from_lo = jnp.where(k < group, rho_g * from_lo + g_ref[k, c], from_lo)
        at_lo = g_ref[groups - 1, 4 + c]
        from_hi = jnp.zeros_like(q)
        for k in range(groups - 1, -1, -1):
            if k < groups - 1:
                at_lo = rho_g * at_lo + g_ref[k, 4 + c]
            from_hi = jnp.where(k > group, rho_g * from_hi + g_ref[k, 4 + c], from_hi)
        x_lo = scale * first * at_lo
        x_hi = scale * at_hi
        if c < 2:
            y_lo = g_ref[0, 8 + c]
            y_hi = g_ref[0, 10 + c]
            for k in range(1, groups):
                y_lo = y_lo + g_ref[k, 8 + c]
                y_hi = y_hi + g_ref[k, 10 + c]
            alpha = (end_s * x_hi - x_lo) * inv_s
            beta = (end_s * x_lo - x_hi) * inv_s
            phi_lo = 2.0 * sinh_s * (x_lo + end_s * beta)
            phi_hi = 2.0 * sinh_s * (x_hi + end_s * alpha)
            w_lo = (2.0 - es) * phi_lo - (2.0 - eq) * (y_lo * inv_pq)
            w_hi = (2.0 - es) * phi_hi - (2.0 - eq) * (y_hi * inv_pq)
            wall_lo = (m_same * w_lo - m_cross * w_hi) * inv_det - x_lo
            wall_hi = (m_same * w_hi - m_cross * w_lo) * inv_det - x_hi
        else:
            wall_lo = -x_lo
            wall_hi = -x_hi
        alpha = (wall_lo - end_s * wall_hi) * inv_s
        beta = (wall_hi - end_s * wall_lo) * inv_s
        t = [scale * v for v in sources(m_ref, c, 4 + c)]
        back = scale * from_hi + beta * far
        falls = [None] * (GRP + 1)
        falls[GRP] = back
        for d in range(GRP - 1, -1, -1):
            back = rho * (back + t[d + 1])
            falls[d] = back
        ahead = scale * from_lo + alpha * near + t[0]
        for d in range(GRP + 1):
            if d:
                ahead = rho * ahead + t[d]
            value = ahead + falls[d]
            if d < GRP:
                o_ref[d, c] = value
            if d:
                o_ref[d - 1, 4 + c] = value


def middle_kernel(s_ref, b_ref, mid_ref, q_ref, own_ref, send_ref):
    core = s_ref[0]

    def tiles(lower, upper):
        @pl.loop(0, GRP)
        def _(i):
            ps = chain(H2 * (q_ref[pl.ds(pl.multiple_of(8 * i, 8), 8), :] + SHIFT), BLK)
            ratio = ps[PTS] / ps[BLK]
            for c in range(4):
                a = b_ref[i, c]
                b = b_ref[i, 4 + c]
                x = ratio * (a + b + mid_ref[i, c])
                lower[i, c] = a
                lower[i, 4 + c] = x
                upper[i, c] = x
                upper[i, 4 + c] = b

    @pl.when(core == 0)
    def _():
        tiles(own_ref, send_ref)

    @pl.when(core != 0)
    def _():
        tiles(send_ref, own_ref)


def points_kernel(s_ref, x_ref, own_ref, r_ref, q_ref, qo_ref, o_ref, buf, sems):
    core = s_ref[0]
    chunks = sems.shape[0]
    per = GRP // chunks

    def half(i, lanes, ends, waves):
        rows = pl.ds(pl.multiple_of(8 * i, 8), 8)
        ps = chain(H2 * (waves[rows, :] + SHIFT), PTS)
        ratio = [None] + [ps[m] / ps[m + 1] for m in range(1, PTS)]
        for c in range(4):
            a = ends[i, c]
            y = [None, KAPPA * x_ref[1, c, rows, lanes] + a]
            for m in range(2, PTS):
                y.append(KAPPA * x_ref[m, c, rows, lanes] + ratio[m - 1] * y[-1])
            buf[0, c, rows, lanes] = a
            value = ends[i, 4 + c]
            for m in range(PTS - 1, 0, -1):
                value = ratio[m] * (y[m] + value)
                buf[m, c, rows, lanes] = value

    def copy(g):
        rows = pl.ds(8 * per * g, 8 * per)
        return pltpu.make_async_copy(buf.at[:, :, rows, :], o_ref.at[:, :, rows, :], sems.at[g])

    for g in range(chunks):
        @pl.when(core == 0)
        def _():
            @pl.loop(per * g, per * (g + 1))
            def _(i):
                half(i, slice(0, 128), own_ref, q_ref)
                half(i, slice(128, 256), r_ref, qo_ref)

        @pl.when(core != 0)
        def _():
            @pl.loop(per * g, per * (g + 1))
            def _(i):
                half(i, slice(0, 128), r_ref, qo_ref)
                half(i, slice(128, 256), own_ref, q_ref)

        copy(g).start()
    for g in range(chunks):
        copy(g).wait()


def in_vmem(value):
    return pltpu.with_memory_space_constraint(value, pltpu.VMEM)


def local_call(kernel, place, operands, shapes):
    return pl.pallas_call(
        kernel,
        in_specs=[pl.BlockSpec(memory_space=pltpu.SMEM)] + [pl.BlockSpec(memory_space=pltpu.VMEM)] * len(operands),
        out_specs=[pl.BlockSpec(memory_space=pltpu.VMEM)] * len(shapes),
        out_shape=[pltpu.VMEM(shape, F32) for shape in shapes],
        compiler_params=pltpu.CompilerParams(vmem_limit_bytes=8 << 20),
    )(place, *[in_vmem(v) for v in operands])


def on_device(forcing, kx_wave, kz_wave):
    ix = lax.axis_index("kx")
    iz = lax.axis_index("kz")
    core = lax.rem(iz, 2)
    chip = iz // 2
    turn = lax.rem(iz - ix + 32, 8)
    place = jnp.stack([core, ix, chip, turn]).astype(jnp.int32)
    both = ("kx", "kz")
    wave_groups = [
        [k * 32 + (k + t) % 8 + 8 * part for k in range(8) for part in range(4)] for t in range(8)
    ]
    core_groups = [[2 * k + c for k in range(GRP)] for c in range(2)]
    pairs = [(i, i ^ 1) for i in range(32)]

    swapped = lax.ppermute(forcing, "kz", pairs)

    part = iz // 8
    kx8 = lax.dynamic_slice_in_dim(kx_wave, 8 * (part // 2), 8).astype(F32)
    sub = lax.broadcasted_iota(jnp.int32, (8, 128), 0)
    payload = jnp.where(
        sub // 4 == lax.rem(part, 2),
        jnp.broadcast_to(kx8[:, None], (8, 128)),
        jnp.broadcast_to(jnp.tile(kz_wave.astype(F32), 16)[None, :], (8, 128)),
    )
    waves = lax.all_to_all(
        jnp.broadcast_to(payload[None], (32, 8, 128)), both, 0, 0, tiled=True, axis_index_groups=wave_groups
    )

    up, mid, q_own, q_oth = local_call(
        moments_kernel, place, (waves, forcing, swapped), ((GRP, 12, 8, 128), (GRP, 4, 8, 128), (128, 128), (128, 128))
    )
    blocks = lax.all_to_all(up, "kz", 0, 0, tiled=True, axis_index_groups=core_groups)
    (message,) = local_call(group_kernel, place, (blocks, q_own), ((8, 12, 8, 128),))
    messages = lax.all_to_all(message, "kx", 0, 0, tiled=True)
    (ends,) = local_call(solve_kernel, place, (blocks, messages, q_own), ((GRP, 8, 8, 128),))
    ends = lax.all_to_all(ends, "kz", 0, 0, tiled=True, axis_index_groups=core_groups)
    own, send = local_call(middle_kernel, place, (ends, mid, q_own), ((GRP, 8, 8, 128),) * 2)
    received = lax.ppermute(send, "kz", pairs)
    return pl.pallas_call(
        points_kernel,
        in_specs=[pl.BlockSpec(memory_space=pltpu.SMEM)] + [pl.BlockSpec(memory_space=pltpu.VMEM)] * 5,
        out_specs=pl.BlockSpec(memory_space=pl.ANY),
        out_shape=jax.ShapeDtypeStruct(forcing.shape, F32),
        scratch_shapes=[pltpu.VMEM(forcing.shape, F32), pltpu.SemaphoreType.DMA((4,))],
        compiler_params=pltpu.CompilerParams(vmem_limit_bytes=8 << 20),
    )(place, *[in_vmem(v) for v in (forcing, own, received, q_own, q_oth)])


def solution(mesh):
    placed = (P(("kx", "kz"), None, None, None), P("kx"), P("kz"))
    return jax.shard_map(
        on_device,
        mesh=mesh,
        in_specs=placed,
        out_specs=P(("kx", "kz"), None, None, None),
        check_vma=False,
    )
```

```python
import functools

import jax
import jax.numpy as jnp
from jax import lax
from jax.experimental import pallas as pl
from jax.experimental.pallas import tpu as pltpu
from jax.sharding import PartitionSpec as P

NY = 1536
N = NY + 1
H2 = (2.0 / N) ** 2
SHIFT = 4000.0
KAPPA = SHIFT * H2
ALPHA_X = 0.25
BETA_Z = 2.0 / 3.0
PTS = 6
BLK = 12
GRP = 16
F32 = jnp.float32


def position():
    ix = lax.axis_index("kx")
    iz = lax.axis_index("kz")
    return lax.rem(iz, 2), ix, lax.div(iz, 2), lax.rem(iz - ix + 32, 8)


def chain(eps, n):
    p = [None, jnp.ones_like(eps)]
    diff = 1.0 + eps
    for _ in range(2, n + 1):
        p.append(p[-1] + diff)
        diff = diff + eps * p[-1]
    return p


def angle(eps):
    x2 = 0.25 * eps
    series = 1.0 + x2 * (-1.0 / 6.0 + x2 * (3.0 / 40.0 + x2 * (-15.0 / 336.0 + x2 * (105.0 / 3456.0))))
    return jnp.sqrt(eps) * series


def waves_kernel(kx_hbm, kz_hbm, o_ref, kx_ref, kz_ref, sems):
    copies = [
        pltpu.make_async_copy(kx_hbm, kx_ref, sems.at[0]),
        pltpu.make_async_copy(kz_hbm, kz_ref, sems.at[1]),
    ]
    for copy in copies:
        copy.start()
    for copy in copies:
        copy.wait()
    part = lax.div(lax.axis_index("kz"), 8)
    sub = lax.broadcasted_iota(jnp.int32, (8, 128), 0)
    lane = lax.rem(lax.broadcasted_iota(jnp.int32, (8, 128), 1), 8)
    kx = jnp.zeros((8, 128), jnp.int32)
    kz = jnp.zeros((8, 128), jnp.int32)
    for r in range(8):
        kx = jnp.where(sub == r, jnp.where(part < 2, kx_ref[r], kx_ref[8 + r]), kx)
        kz = jnp.where(lane == r, kz_ref[r], kz)
    row = jnp.where(lax.div(sub, 4) == lax.rem(part, 2), kx, kz).astype(F32)
    for j in range(o_ref.shape[0]):
        o_ref[j] = row


def moments_kernel(w_ref, x_ref, r_ref, up_ref, mid_ref, q_ref, qo_ref, ratio_ref, x_own, sems):
    core, _, _, turn = position()
    chunks = sems.shape[0]
    per = GRP // chunks

    def copy(g, half):
        rows = pl.ds(8 * per * g, 8 * per)
        return pltpu.make_async_copy(
            x_ref.at[:, :, rows, pl.ds(128 * half, 128)], x_own.at[:, :, rows, :], sems.at[g]
        )

    for half in range(2):
        @pl.when(core == half)
        def _():
            for g in range(chunks):
                copy(g, half).start()

    lane = lax.broadcasted_iota(jnp.int32, (8, 128), 1) // 8
    sub = lax.broadcasted_iota(jnp.int32, (8, 128), 0)

    def kz_row(half):
        acc = [jnp.zeros((8, 128), F32), jnp.zeros((8, 128), F32)]
        for j in range(32):
            place = lax.rem(j // 4 + turn, 8) + 8 * (j % 4) - GRP * half
            acc[j % 2] = acc[j % 2] + jnp.where(lane == place, w_ref[j], 0.0)
        row = acc[0][4:5, :] + acc[1][0:1, :]
        return (BETA_Z * jnp.broadcast_to(row, (8, 128))) ** 2

    kz_own = kz_row(core)
    kz_oth = kz_row(1 - core)

    def tiles(g, first, second):
        @pl.loop(per * g, per * (g + 1), unroll=2)
        def _(i):
            kx = (ALPHA_X * jnp.where(sub < 4, w_ref[2 * i], w_ref[2 * i + 1])) ** 2
            rows = pl.ds(pl.multiple_of(8 * i, 8), 8)
            q = kx + kz_own
            q_ref[rows, :] = q
            qo_ref[rows, :] = kx + kz_oth
            ps = chain(H2 * (q + SHIFT), BLK)
            pq = chain(H2 * q, BLK)
            ratio = ps[PTS] / ps[BLK]
            ratio_ref[rows, :] = ratio
            for c in range(4):
                f = [first(m, c, rows) for m in range(PTS)] + [second(m, c, rows) for m in range(PTS)]
                own = ps[BLK] * f[0]
                nxt = ps[1] * f[1]
                mid = ps[1] * f[1]
                for m in range(1, BLK):
                    own = own + ps[BLK - m] * f[m]
                for m in range(2, BLK):
                    nxt = nxt + ps[m] * f[m]
                    mid = mid + ps[min(m, BLK - m)] * f[m]
                up_ref[i, c] = KAPPA * own
                up_ref[i, 4 + c] = KAPPA * nxt
                mid_ref[i, c] = ratio * (KAPPA * mid)
                if c < 2:
                    own = pq[BLK] * f[0]
                    nxt = pq[1] * f[1]
                    for m in range(1, BLK):
                        own = own + pq[BLK - m] * f[m]
                    for m in range(2, BLK):
                        nxt = nxt + pq[m] * f[m]
                    up_ref[i, 8 + c] = KAPPA * own
                    up_ref[i, 10 + c] = KAPPA * nxt

    for g in range(chunks):
        copy(g, 0).wait()

        @pl.when(core == 0)
        def _():
            tiles(g, lambda m, c, rows: x_own[m, c, rows, :], lambda m, c, rows: r_ref[m, c, rows, :128])

        @pl.when(core != 0)
        def _():
            tiles(g, lambda m, c, rows: r_ref[m, c, rows, 128:], lambda m, c, rows: x_own[m, c, rows, :])


def sources(m_ref, own, nxt):
    return (
        [m_ref[0, own]]
        + [m_ref[d, own] + m_ref[d - 1, nxt] for d in range(1, GRP)]
        + [m_ref[GRP - 1, nxt]]
    )


def group_kernel(m_ref, q_ref, o_ref):
    _, group, chip, _ = position()
    q = q_ref[pl.ds(pl.multiple_of(8 * chip, 8), 8), :]
    rho = jnp.exp(-BLK * angle(H2 * (q + SHIFT)))
    res = [None] * 12
    for c in range(4):
        t = sources(m_ref, c, 4 + c)
        right = t[0]
        for d in range(1, GRP + 1):
            right = rho * right + t[d]
        left = t[GRP]
        for d in range(GRP - 1, -1, -1):
            left = rho * left + t[d]
        res[c] = right
        res[4 + c] = left
    tq = angle(H2 * q)
    end = jnp.exp(-N * tq)
    inv = 1.0 / jnp.where(q > 0.0, 1.0 - end * end, 1.0)
    sq = [sources(m_ref, 8 + c, 10 + c) for c in range(2)]
    for c in range(2):
        res[8 + c] = jnp.zeros_like(q)
        res[10 + c] = jnp.zeros_like(q)
    for d in range(GRP + 1):
        place = (BLK * (GRP * group + d) + 1).astype(F32)
        fall = jnp.exp(-place * tq)
        rise = (jnp.exp((place - N) * tq) - end * fall) * inv
        rise = jnp.where(q > 0.0, rise, place * (1.0 / N))
        fall = fall - end * rise
        for c in range(2):
            res[8 + c] = res[8 + c] + fall * sq[c][d]
            res[10 + c] = res[10 + c] + rise * sq[c][d]
    for k in range(o_ref.shape[0]):
        for n in range(12):
            o_ref[k, n] = res[n]


def solve_kernel(m_ref, g_ref, q_ref, o_ref):
    _, group, chip, _ = position()
    groups = g_ref.shape[0]
    q = q_ref[pl.ds(pl.multiple_of(8 * chip, 8), 8), :]
    es = H2 * (q + SHIFT)
    eq = H2 * q
    ts = angle(es)
    tq = angle(eq)
    rho = jnp.exp(-BLK * ts)
    rho_g = jnp.exp(-(BLK * GRP) * ts)
    sinh_s = jnp.sqrt(es * (1.0 + 0.25 * es))
    sinh_q = jnp.sqrt(eq * (1.0 + 0.25 * eq))
    scale = 0.5 / (sinh_s * chain(es, BLK)[BLK])
    end_s = jnp.exp(-N * ts)
    inv_s = 1.0 / (1.0 - end_s * end_s)
    end_q = jnp.exp(-N * tq)
    positive = q > 0.0
    inv_q = 1.0 / jnp.where(positive, 1.0 - end_q * end_q, 1.0)
    coth_s = sinh_s * (1.0 + end_s * end_s) * inv_s
    csch_s = 2.0 * sinh_s * end_s * inv_s
    coth_q = jnp.where(positive, sinh_q * (1.0 + end_q * end_q) * inv_q, 1.0 / N)
    csch_q = jnp.where(positive, 2.0 * sinh_q * end_q * inv_q, 1.0 / N)
    m_same = (2.0 - es) * coth_s - (2.0 - eq) * coth_q + 0.5 * (es * es - eq * eq)
    m_cross = (2.0 - eq) * csch_q - (2.0 - es) * csch_s
    inv_det = 1.0 / (m_same * m_same - m_cross * m_cross)
    inv_pq = 1.0 / chain(eq, BLK)[BLK]
    gf = group.astype(F32)
    near = jnp.exp(-(gf * (BLK * GRP) + 1.0) * ts)
    far = jnp.exp(-(NY - BLK * GRP - gf * (BLK * GRP)) * ts)
    first = jnp.exp(-ts)
    for c in range(4):
        at_hi = g_ref[0, c]
        from_lo = jnp.zeros_like(q)
        for k in range(groups):
            if k:
                at_hi = rho_g * at_hi + g_ref[k, c]
            from_lo = jnp.where(k < group, rho_g * from_lo + g_ref[k, c], from_lo)
        at_lo = g_ref[groups - 1, 4 + c]
        from_hi = jnp.zeros_like(q)
        for k in range(groups - 1, -1, -1):
            if k < groups - 1:
                at_lo = rho_g * at_lo + g_ref[k, 4 + c]
            from_hi = jnp.where(k > group, rho_g * from_hi + g_ref[k, 4 + c], from_hi)
        x_lo = scale * first * at_lo
        x_hi = scale * at_hi
        if c < 2:
            y_lo = g_ref[0, 8 + c]
            y_hi = g_ref[0, 10 + c]
            for k in range(1, groups):
                y_lo = y_lo + g_ref[k, 8 + c]
                y_hi = y_hi + g_ref[k, 10 + c]
            alpha = (end_s * x_hi - x_lo) * inv_s
            beta = (end_s * x_lo - x_hi) * inv_s
            phi_lo = 2.0 * sinh_s * (x_lo + end_s * beta)
            phi_hi = 2.0 * sinh_s * (x_hi + end_s * alpha)
            w_lo = (2.0 - es) * phi_lo - (2.0 - eq) * (y_lo * inv_pq)
            w_hi = (2.0 - es) * phi_hi - (2.0 - eq) * (y_hi * inv_pq)
            wall_lo = (m_same * w_lo - m_cross * w_hi) * inv_det - x_lo
            wall_hi = (m_same * w_hi - m_cross * w_lo) * inv_det - x_hi
        else:
            wall_lo = -x_lo
            wall_hi = -x_hi
        alpha = (wall_lo - end_s * wall_hi) * inv_s
        beta = (wall_hi - end_s * wall_lo) * inv_s
        t = [scale * v for v in sources(m_ref, c, 4 + c)]
        back = scale * from_hi + beta * far
        falls = [None] * (GRP + 1)
        falls[GRP] = back
        for d in range(GRP - 1, -1, -1):
            back = rho * (back + t[d + 1])
            falls[d] = back
        ahead = scale * from_lo + alpha * near + t[0]
        for d in range(GRP + 1):
            if d:
                ahead = rho * ahead + t[d]
            value = ahead + falls[d]
            if d < GRP:
                o_ref[d, c] = value
            if d:
                o_ref[d - 1, 4 + c] = value


def middle_kernel(b_ref, mid_ref, ratio_ref, own_ref, send_ref):
    core, _, _, _ = position()

    def tiles(lower, upper):
        @pl.loop(0, GRP, unroll=2)
        def _(i):
            ratio = ratio_ref[pl.ds(pl.multiple_of(8 * i, 8), 8), :]
            for c in range(4):
                a = b_ref[i, c]
                b = b_ref[i, 4 + c]
                x = ratio * (a + b) + mid_ref[i, c]
                lower[i, c] = a
                lower[i, 4 + c] = x
                upper[i, c] = x
                upper[i, 4 + c] = b

    @pl.when(core == 0)
    def _():
        tiles(own_ref, send_ref)

    @pl.when(core != 0)
    def _():
        tiles(send_ref, own_ref)


def points_kernel(other, x_ref, ends, q_ref, *refs):
    o_ref, buf, sems = refs[-3:]
    core, _, _, _ = position()
    chunks = sems.shape[0]
    per = GRP // chunks

    def tile(i, lanes):
        rows = pl.ds(pl.multiple_of(8 * i, 8), 8)
        ps = chain(H2 * (q_ref[rows, :] + SHIFT), PTS)
        ratio = [None] + [ps[m] / ps[m + 1] for m in range(1, PTS)]
        for c in range(4):
            a = ends[i, c]
            y = [None, KAPPA * x_ref[1, c, rows, lanes] + a]
            for m in range(2, PTS):
                y.append(KAPPA * x_ref[m, c, rows, lanes] + ratio[m - 1] * y[-1])
            buf[0, c, rows, :] = a
            value = ends[i, 4 + c]
            for m in range(PTS - 1, 0, -1):
                value = ratio[m] * (y[m] + value)
                buf[m, c, rows, :] = value

    def copy(g, half):
        rows = pl.ds(8 * per * g, 8 * per)
        return pltpu.make_async_copy(
            buf.at[:, :, rows, :], o_ref.at[:, :, rows, pl.ds(128 * half, 128)], sems.at[g]
        )

    for half in range(2):
        @pl.when(core == (1 - half if other else half))
        def _():
            for g in range(chunks):
                @pl.loop(per * g, per * (g + 1), unroll=2)
                def _(i):
                    tile(i, slice(128 * half, 128 * half + 128))

                copy(g, half).start()

    for g in range(chunks):
        copy(g, 0).wait()


def in_vmem(value):
    return pltpu.with_memory_space_constraint(value, pltpu.VMEM)


def local_call(kernel, operands, shapes):
    return pl.pallas_call(
        kernel,
        in_specs=[pl.BlockSpec(memory_space=pltpu.VMEM)] * len(operands),
        out_specs=[pl.BlockSpec(memory_space=pltpu.VMEM)] * len(shapes),
        out_shape=[pltpu.VMEM(shape, F32) for shape in shapes],
        compiler_params=pltpu.CompilerParams(vmem_limit_bytes=8 << 20),
    )(*[in_vmem(v) for v in operands])


def on_device(forcing, kx_wave, kz_wave):
    both = ("kx", "kz")
    wave_groups = [
        [k * 32 + (k + t) % 8 + 8 * part for k in range(8) for part in range(4)] for t in range(8)
    ]
    core_groups = [[2 * k + c for k in range(GRP)] for c in range(2)]
    pairs = [(i, i ^ 1) for i in range(32)]

    vmem = pl.BlockSpec(memory_space=pltpu.VMEM)
    hbm = pl.BlockSpec(memory_space=pltpu.HBM)
    params = pltpu.CompilerParams(vmem_limit_bytes=8 << 20)
    half_shape = (PTS, 4, 128, 128)

    swapped = lax.ppermute(forcing, "kz", pairs)

    payload = pl.pallas_call(
        waves_kernel,
        in_specs=[hbm] * 2,
        out_specs=vmem,
        out_shape=pltpu.VMEM((32, 8, 128), F32),
        scratch_shapes=[
            pltpu.SMEM(kx_wave.shape, jnp.int32),
            pltpu.SMEM(kz_wave.shape, jnp.int32),
            pltpu.SemaphoreType.DMA((2,)),
        ],
        compiler_params=params,
    )(*[pltpu.with_memory_space_constraint(v, pltpu.HBM) for v in (kx_wave, kz_wave)])
    waves = lax.all_to_all(payload, both, 0, 0, tiled=True, axis_index_groups=wave_groups)
    up, mid, q_own, q_oth, ratio = pl.pallas_call(
        moments_kernel,
        in_specs=[vmem, hbm, vmem],
        out_specs=[vmem] * 5,
        out_shape=[
            pltpu.VMEM(shape, F32)
            for shape in ((GRP, 12, 8, 128), (GRP, 4, 8, 128), (128, 128), (128, 128), (128, 128))
        ],
        scratch_shapes=[pltpu.VMEM(half_shape, F32), pltpu.SemaphoreType.DMA((4,))],
        compiler_params=params,
    )(in_vmem(waves), pltpu.with_memory_space_constraint(forcing, pltpu.HBM), in_vmem(swapped))
    blocks = lax.all_to_all(up, "kz", 0, 0, tiled=True, axis_index_groups=core_groups)
    (message,) = local_call(group_kernel, (blocks, q_own), ((8, 12, 8, 128),))
    messages = lax.all_to_all(message, "kx", 0, 0, tiled=True)
    (ends,) = local_call(solve_kernel, (blocks, messages, q_own), ((GRP, 8, 8, 128),))
    ends = lax.all_to_all(ends, "kz", 0, 0, tiled=True, axis_index_groups=core_groups)
    own, send = local_call(middle_kernel, (ends, mid, ratio), ((GRP, 8, 8, 128),) * 2)
    received = lax.ppermute(send, "kz", pairs)

    def points(other, operands, *made):
        return pl.pallas_call(
            functools.partial(points_kernel, other),
            in_specs=[vmem] * 3 + [hbm] * len(made),
            out_specs=hbm,
            out_shape=pltpu.HBM(forcing.shape, F32),
            input_output_aliases={3: 0} if made else {},
            scratch_shapes=[pltpu.VMEM(half_shape, F32), pltpu.SemaphoreType.DMA((4,))],
            compiler_params=params,
            cost_estimate=pl.CostEstimate(flops=8 << 20, bytes_accessed=4 << 20, transcendentals=0),
        )(*[in_vmem(v) for v in operands], *made)

    fields = points(False, (forcing, own, q_own))
    return points(True, (forcing, received, q_oth), fields)


def solution(mesh):
    placed = (P(("kx", "kz"), None, None, None), P("kx"), P("kz"))
    return jax.shard_map(
        on_device,
        mesh=mesh,
        in_specs=placed,
        out_specs=P(("kx", "kz"), None, None, None),
        check_vma=False,
    )
```

```python
import functools

import jax
import jax.numpy as jnp
from jax import lax
from jax.experimental import pallas as pl
from jax.experimental.pallas import tpu as pltpu
from jax.sharding import PartitionSpec as P

NY = 1536
N = NY + 1
H2 = (2.0 / N) ** 2
SHIFT = 4000.0
KAPPA = SHIFT * H2
ALPHA_X = 0.25
BETA_Z = 2.0 / 3.0
PTS = 6
BLK = 12
GRP = 16
F32 = jnp.float32


def position():
    iz = lax.axis_index("kz")
    return lax.rem(iz, 2), lax.axis_index("kx"), lax.div(iz, 2)


def wave_group():
    ix = lax.axis_index("kx")
    iz = lax.axis_index("kz")
    x_lo, y = lax.div(ix, 4), lax.rem(ix, 4)
    z, x_hi = lax.div(iz, 4), lax.rem(lax.div(iz, 2), 2)
    return lax.rem(y - z + 8, 4), lax.rem(x_lo + x_hi + lax.div(z, 4), 2)


def wave_member(j, ty, tx):
    x_lo, y, b, core = j // 16, j // 4 % 4, j // 2 % 2, j % 2
    return 4 * ((y - ty + 4) % 4 + 4 * b) + 2 * ((x_lo + tx + b) % 2) + core


def chain(eps, n):
    p = [None, jnp.ones_like(eps)]
    diff = 1.0 + eps
    for _ in range(2, n + 1):
        p.append(p[-1] + diff)
        diff = diff + eps * p[-1]
    return p


def angle(eps):
    x2 = 0.25 * eps
    series = 1.0 + x2 * (-1.0 / 6.0 + x2 * (3.0 / 40.0 + x2 * (-15.0 / 336.0 + x2 * (105.0 / 3456.0))))
    return jnp.sqrt(eps) * series


def waves_kernel(kx_hbm, kz_hbm, o_ref, kx_ref, kz_ref, sems):
    copies = [
        pltpu.make_async_copy(kx_hbm, kx_ref, sems.at[0]),
        pltpu.make_async_copy(kz_hbm, kz_ref, sems.at[1]),
    ]
    for copy in copies:
        copy.start()
    for copy in copies:
        copy.wait()
    iz = lax.axis_index("kz")
    part = 2 * lax.div(iz, 16) + lax.rem(iz, 2)
    lane = lax.broadcasted_iota(jnp.int32, (2, 128), 1)
    kx = jnp.zeros((2, 128), jnp.int32)
    kz = jnp.zeros((2, 128), jnp.int32)
    for r in range(4):
        kx = jnp.where(lax.rem(lane, 4) == r, kx_ref[4 * part + r], kx)
    for r in range(8):
        kz = jnp.where(lax.rem(lane, 8) == r, kz_ref[r], kz)
    rows = jnp.where(lax.broadcasted_iota(jnp.int32, (2, 128), 0) == 0, kz, kx).astype(F32)
    for j in range(o_ref.shape[0]):
        o_ref[j] = rows


def moments_kernel(w_ref, x_ref, r_ref, up_ref, mid_ref, q_ref, qo_ref, ratio_ref, x_own, sems):
    core, _, _ = position()
    ty, tx = wave_group()
    chunks = sems.shape[0]
    per = GRP // chunks

    def copy(g, half):
        rows = pl.ds(8 * per * g, 8 * per)
        return pltpu.make_async_copy(
            x_ref.at[:, :, rows, pl.ds(128 * half, 128)], x_own.at[:, :, rows, :], sems.at[g]
        )

    for half in range(2):
        @pl.when(core == half)
        def _():
            for g in range(chunks):
                copy(g, half).start()

    lane = lax.broadcasted_iota(jnp.int32, (8, 128), 1)
    sub = lax.broadcasted_iota(jnp.int32, (8, 128), 0)
    places = [wave_member(j, ty, tx) for j in range(32)]

    def kz_row(half):
        acc = [jnp.zeros((1, 128), F32) for _ in range(4)]
        for j in range(32):
            acc[j % 4] = jnp.where(lane[0:1] // 8 == places[j] - GRP * half, w_ref[j, 0:1, :], acc[j % 4])
        row = (acc[0] + acc[1]) + (acc[2] + acc[3])
        return (BETA_Z * jnp.broadcast_to(row, (8, 128))) ** 2

    def kx_column(i):
        rows = jnp.where(sub < 4, w_ref[2 * i, 1:2, :], w_ref[2 * i + 1, 1:2, :])
        column = jnp.sum(jnp.where(lane == lax.rem(sub, 4), rows, 0.0), axis=1, keepdims=True)
        return (ALPHA_X * jnp.broadcast_to(column, (8, 128))) ** 2

    kz_own = kz_row(core)
    kz_oth = kz_row(1 - core)
    for i in range(GRP):
        kx = kx_column(i)
        q_ref[8 * i : 8 * i + 8, :] = kx + kz_own
        qo_ref[8 * i : 8 * i + 8, :] = kx + kz_oth

    def tiles(g, first, second):
        @pl.loop(per * g, per * (g + 1), unroll=2)
        def _(i):
            rows = pl.ds(pl.multiple_of(8 * i, 8), 8)
            q = q_ref[rows, :]
            ps = chain(H2 * (q + SHIFT), BLK)
            pq = chain(H2 * q, BLK)
            ratio = ps[PTS] / ps[BLK]
            ratio_ref[rows, :] = ratio
            for c in range(4):
                f = [first(m, c, rows) for m in range(PTS)] + [second(m, c, rows) for m in range(PTS)]
                own = ps[BLK] * f[0]
                nxt = jnp.zeros_like(own)
                mid = jnp.zeros_like(own)
                for m in range(1, BLK):
                    to_own = ps[BLK - m] * f[m]
                    to_nxt = ps[m] * f[m]
                    own = own + to_own
                    nxt = nxt + to_nxt
                    mid = mid + (to_nxt if m <= PTS else to_own)
                up_ref[i, c] = KAPPA * own
                up_ref[i, 4 + c] = KAPPA * nxt
                mid_ref[i, c] = ratio * (KAPPA * mid)
                if c < 2:
                    own = pq[BLK] * f[0]
                    nxt = pq[1] * f[1]
                    for m in range(1, BLK):
                        own = own + pq[BLK - m] * f[m]
                    for m in range(2, BLK):
                        nxt = nxt + pq[m] * f[m]
                    up_ref[i, 8 + c] = KAPPA * own
                    up_ref[i, 10 + c] = KAPPA * nxt

    for g in range(chunks):
        copy(g, 0).wait()

        @pl.when(core == 0)
        def _():
            tiles(g, lambda m, c, rows: x_own[m, c, rows, :], lambda m, c, rows: r_ref[m, c, rows, :128])

        @pl.when(core != 0)
        def _():
            tiles(g, lambda m, c, rows: r_ref[m, c, rows, 128:], lambda m, c, rows: x_own[m, c, rows, :])


def sources(m_ref, own, nxt):
    return (
        [m_ref[0, own]]
        + [m_ref[d, own] + m_ref[d - 1, nxt] for d in range(1, GRP)]
        + [m_ref[GRP - 1, nxt]]
    )


def group_kernel(m_ref, q_ref, o_ref):
    _, group, chip = position()
    q = q_ref[pl.ds(pl.multiple_of(8 * chip, 8), 8), :]
    rho = jnp.exp(-BLK * angle(H2 * (q + SHIFT)))
    res = [None] * 12
    for c in range(4):
        t = sources(m_ref, c, 4 + c)
        right = t[0]
        for d in range(1, GRP + 1):
            right = rho * right + t[d]
        left = t[GRP]
        for d in range(GRP - 1, -1, -1):
            left = rho * left + t[d]
        res[c] = right
        res[4 + c] = left
    tq = angle(H2 * q)
    end = jnp.exp(-N * tq)
    inv = 1.0 / jnp.where(q > 0.0, 1.0 - end * end, 1.0)
    sq = [sources(m_ref, 8 + c, 10 + c) for c in range(2)]
    for c in range(2):
        res[8 + c] = jnp.zeros_like(q)
        res[10 + c] = jnp.zeros_like(q)
    for d in range(GRP + 1):
        place = (BLK * (GRP * group + d) + 1).astype(F32)
        fall = jnp.exp(-place * tq)
        rise = (jnp.exp((place - N) * tq) - end * fall) * inv
        rise = jnp.where(q > 0.0, rise, place * (1.0 / N))
        fall = fall - end * rise
        for c in range(2):
            res[8 + c] = res[8 + c] + fall * sq[c][d]
            res[10 + c] = res[10 + c] + rise * sq[c][d]
    for k in range(o_ref.shape[0]):
        for n in range(12):
            o_ref[k, n] = res[n]


def solve_kernel(m_ref, g_ref, q_ref, o_ref):
    _, group, chip = position()
    groups = g_ref.shape[0]
    q = q_ref[pl.ds(pl.multiple_of(8 * chip, 8), 8), :]
    es = H2 * (q + SHIFT)
    eq = H2 * q
    ts = angle(es)
    tq = angle(eq)
    rho = jnp.exp(-BLK * ts)
    rho_g = jnp.exp(-(BLK * GRP) * ts)
    sinh_s = jnp.sqrt(es * (1.0 + 0.25 * es))
    sinh_q = jnp.sqrt(eq * (1.0 + 0.25 * eq))
    scale = 0.5 / (sinh_s * chain(es, BLK)[BLK])
    end_s = jnp.exp(-N * ts)
    inv_s = 1.0 / (1.0 - end_s * end_s)
    end_q = jnp.exp(-N * tq)
    positive = q > 0.0
    inv_q = 1.0 / jnp.where(positive, 1.0 - end_q * end_q, 1.0)
    coth_s = sinh_s * (1.0 + end_s * end_s) * inv_s
    csch_s = 2.0 * sinh_s * end_s * inv_s
    coth_q = jnp.where(positive, sinh_q * (1.0 + end_q * end_q) * inv_q, 1.0 / N)
    csch_q = jnp.where(positive, 2.0 * sinh_q * end_q * inv_q, 1.0 / N)
    m_same = (2.0 - es) * coth_s - (2.0 - eq) * coth_q + 0.5 * (es * es - eq * eq)
    m_cross = (2.0 - eq) * csch_q - (2.0 - es) * csch_s
    inv_det = 1.0 / (m_same * m_same - m_cross * m_cross)
    inv_pq = 1.0 / chain(eq, BLK)[BLK]
    gf = group.astype(F32)
    near = jnp.exp(-(gf * (BLK * GRP) + 1.0) * ts)
    far = jnp.exp(-(NY - BLK * GRP - gf * (BLK * GRP)) * ts)
    first = jnp.exp(-ts)
    for c in range(4):
        at_hi = g_ref[0, c]
        from_lo = jnp.zeros_like(q)
        for k in range(groups):
            if k:
                at_hi = rho_g * at_hi + g_ref[k, c]
            from_lo = jnp.where(k < group, rho_g * from_lo + g_ref[k, c], from_lo)
        at_lo = g_ref[groups - 1, 4 + c]
        from_hi = jnp.zeros_like(q)
        for k in range(groups - 1, -1, -1):
            if k < groups - 1:
                at_lo = rho_g * at_lo + g_ref[k, 4 + c]
            from_hi = jnp.where(k > group, rho_g * from_hi + g_ref[k, 4 + c], from_hi)
        x_lo = scale * first * at_lo
        x_hi = scale * at_hi
        if c < 2:
            y_lo = g_ref[0, 8 + c]
            y_hi = g_ref[0, 10 + c]
            for k in range(1, groups):
                y_lo = y_lo + g_ref[k, 8 + c]
                y_hi = y_hi + g_ref[k, 10 + c]
            alpha = (end_s * x_hi - x_lo) * inv_s
            beta = (end_s * x_lo - x_hi) * inv_s
            phi_lo = 2.0 * sinh_s * (x_lo + end_s * beta)
            phi_hi = 2.0 * sinh_s * (x_hi + end_s * alpha)
            w_lo = (2.0 - es) * phi_lo - (2.0 - eq) * (y_lo * inv_pq)
            w_hi = (2.0 - es) * phi_hi - (2.0 - eq) * (y_hi * inv_pq)
            wall_lo = (m_same * w_lo - m_cross * w_hi) * inv_det - x_lo
            wall_hi = (m_same * w_hi - m_cross * w_lo) * inv_det - x_hi
        else:
            wall_lo = -x_lo
            wall_hi = -x_hi
        alpha = (wall_lo - end_s * wall_hi) * inv_s
        beta = (wall_hi - end_s * wall_lo) * inv_s
        t = [scale * v for v in sources(m_ref, c, 4 + c)]
        back = scale * from_hi + beta * far
        falls = [None] * (GRP + 1)
        falls[GRP] = back
        for d in range(GRP - 1, -1, -1):
            back = rho * (back + t[d + 1])
            falls[d] = back
        ahead = scale * from_lo + alpha * near + t[0]
        for d in range(GRP + 1):
            if d:
                ahead = rho * ahead + t[d]
            value = ahead + falls[d]
            if d < GRP:
                o_ref[d, c] = value
            if d:
                o_ref[d - 1, 4 + c] = value


def middle_kernel(b_ref, mid_ref, ratio_ref, own_ref, send_ref):
    core, _, _ = position()

    def tiles(lower, upper):
        @pl.loop(0, GRP, unroll=2)
        def _(i):
            ratio = ratio_ref[pl.ds(pl.multiple_of(8 * i, 8), 8), :]
            for c in range(4):
                a = b_ref[i, c]
                b = b_ref[i, 4 + c]
                x = ratio * (a + b) + mid_ref[i, c]
                lower[i, c] = a
                lower[i, 4 + c] = x
                upper[i, c] = x
                upper[i, 4 + c] = b

    @pl.when(core == 0)
    def _():
        tiles(own_ref, send_ref)

    @pl.when(core != 0)
    def _():
        tiles(send_ref, own_ref)


def points_kernel(other, x_ref, ends, q_ref, *refs):
    o_ref, buf, sems = refs[-3:]
    core, _, _ = position()
    chunks = sems.shape[0]
    per = GRP // chunks

    def tile(i, lanes):
        rows = pl.ds(pl.multiple_of(8 * i, 8), 8)
        ps = chain(H2 * (q_ref[rows, :] + SHIFT), PTS)
        ratio = [None] + [ps[m] / ps[m + 1] for m in range(1, PTS)]
        for c in range(4):
            a = ends[i, c]
            y = [None, KAPPA * x_ref[1, c, rows, lanes] + a]
            for m in range(2, PTS):
                y.append(KAPPA * x_ref[m, c, rows, lanes] + ratio[m - 1] * y[-1])
            buf[0, c, rows, :] = a
            value = ends[i, 4 + c]
            for m in range(PTS - 1, 0, -1):
                value = ratio[m] * (y[m] + value)
                buf[m, c, rows, :] = value

    def copy(g, half):
        rows = pl.ds(8 * per * g, 8 * per)
        return pltpu.make_async_copy(
            buf.at[:, :, rows, :], o_ref.at[:, :, rows, pl.ds(128 * half, 128)], sems.at[g]
        )

    for half in range(2):
        @pl.when(core == (1 - half if other else half))
        def _():
            for g in range(chunks):
                @pl.loop(per * g, per * (g + 1), unroll=2)
                def _(i):
                    tile(i, slice(128 * half, 128 * half + 128))

                copy(g, half).start()

    for g in range(chunks):
        copy(g, 0).wait()


def in_vmem(value):
    return pltpu.with_memory_space_constraint(value, pltpu.VMEM)


def local_call(kernel, operands, shapes):
    return pl.pallas_call(
        kernel,
        in_specs=[pl.BlockSpec(memory_space=pltpu.VMEM)] * len(operands),
        out_specs=[pl.BlockSpec(memory_space=pltpu.VMEM)] * len(shapes),
        out_shape=[pltpu.VMEM(shape, F32) for shape in shapes],
        compiler_params=pltpu.CompilerParams(vmem_limit_bytes=8 << 20),
    )(*[in_vmem(v) for v in operands])


def on_device(forcing, kx_wave, kz_wave):
    both = ("kx", "kz")
    wave_groups = [
        [32 * (j // 4) + wave_member(j, ty, tx) for j in range(32)] for ty in range(4) for tx in range(2)
    ]
    core_groups = [[2 * k + c for k in range(GRP)] for c in range(2)]
    pairs = [(i, i ^ 1) for i in range(32)]

    vmem = pl.BlockSpec(memory_space=pltpu.VMEM)
    hbm = pl.BlockSpec(memory_space=pltpu.HBM)
    params = pltpu.CompilerParams(vmem_limit_bytes=8 << 20)
    half_shape = (PTS, 4, 128, 128)

    swapped = lax.ppermute(forcing, "kz", pairs)

    payload = pl.pallas_call(
        waves_kernel,
        in_specs=[hbm] * 2,
        out_specs=vmem,
        out_shape=pltpu.VMEM((32, 2, 128), F32),
        scratch_shapes=[
            pltpu.SMEM(kx_wave.shape, jnp.int32),
            pltpu.SMEM(kz_wave.shape, jnp.int32),
            pltpu.SemaphoreType.DMA((2,)),
        ],
        compiler_params=params,
    )(*[pltpu.with_memory_space_constraint(v, pltpu.HBM) for v in (kx_wave, kz_wave)])
    waves = lax.all_to_all(payload, both, 0, 0, tiled=True, axis_index_groups=wave_groups)
    up, mid, q_own, q_oth, ratio = pl.pallas_call(
        moments_kernel,
        in_specs=[vmem, hbm, vmem],
        out_specs=[vmem] * 5,
        out_shape=[
            pltpu.VMEM(shape, F32)
            for shape in ((GRP, 12, 8, 128), (GRP, 4, 8, 128), (128, 128), (128, 128), (128, 128))
        ],
        scratch_shapes=[pltpu.VMEM(half_shape, F32), pltpu.SemaphoreType.DMA((4,))],
        compiler_params=params,
    )(in_vmem(waves), pltpu.with_memory_space_constraint(forcing, pltpu.HBM), in_vmem(swapped))
    blocks = lax.all_to_all(up, "kz", 0, 0, tiled=True, axis_index_groups=core_groups)
    (message,) = local_call(group_kernel, (blocks, q_own), ((8, 12, 8, 128),))
    messages = lax.all_to_all(message, "kx", 0, 0, tiled=True)
    (ends,) = local_call(solve_kernel, (blocks, messages, q_own), ((GRP, 8, 8, 128),))
    ends = lax.all_to_all(ends, "kz", 0, 0, tiled=True, axis_index_groups=core_groups)
    own, send = local_call(middle_kernel, (ends, mid, ratio), ((GRP, 8, 8, 128),) * 2)
    received = lax.ppermute(send, "kz", pairs)

    def points(other, operands, *made):
        return pl.pallas_call(
            functools.partial(points_kernel, other),
            in_specs=[vmem] * 3 + [hbm] * len(made),
            out_specs=hbm,
            out_shape=pltpu.HBM(forcing.shape, F32),
            input_output_aliases={3: 0} if made else {},
            scratch_shapes=[pltpu.VMEM(half_shape, F32), pltpu.SemaphoreType.DMA((4,))],
            compiler_params=params,
            cost_estimate=pl.CostEstimate(flops=8 << 20, bytes_accessed=4 << 20, transcendentals=0),
        )(*[in_vmem(v) for v in operands], *made)

    fields = points(False, (forcing, own, q_own))
    return points(True, (forcing, received, q_oth), fields)


def solution(mesh):
    placed = (P(("kx", "kz"), None, None, None), P("kx"), P("kz"))
    return jax.shard_map(
        on_device,
        mesh=mesh,
        in_specs=placed,
        out_specs=P(("kx", "kz"), None, None, None),
        check_vma=False,
    )
```

```python
import functools

import jax
import jax.numpy as jnp
from jax import lax
from jax.experimental import pallas as pl
from jax.experimental.pallas import tpu as pltpu
from jax.sharding import PartitionSpec as P

NY = 1536
N = NY + 1
H2 = (2.0 / N) ** 2
SHIFT = 4000.0
KAPPA = SHIFT * H2
ALPHA_X = 0.25
BETA_Z = 2.0 / 3.0
PTS = 6
BLK = 12
GRP = 16
CHIPS = 128
NUM = 12
F32 = jnp.float32


def position():
    iz = lax.axis_index("kz")
    return lax.rem(iz, 2), lax.axis_index("kx"), lax.div(iz, 2)


def wave_group():
    ix = lax.axis_index("kx")
    iz = lax.axis_index("kz")
    x_lo, y = lax.div(ix, 4), lax.rem(ix, 4)
    z, x_hi = lax.div(iz, 4), lax.rem(lax.div(iz, 2), 2)
    return lax.rem(y - z + 8, 4), lax.rem(x_lo + x_hi + lax.div(z, 4), 2)


def wave_member(j, ty, tx):
    x_lo, y, b, core = j // 16, j // 4 % 4, j // 2 % 2, j % 2
    return 4 * ((y - ty + 4) % 4 + 4 * b) + 2 * ((x_lo + tx + b) % 2) + core


def chain(eps, n):
    p = [None, jnp.ones_like(eps)]
    diff = 1.0 + eps
    for _ in range(2, n + 1):
        p.append(p[-1] + diff)
        diff = diff + eps * p[-1]
    return p


def angle(eps):
    x2 = 0.25 * eps
    series = 1.0 + x2 * (-1.0 / 6.0 + x2 * (3.0 / 40.0 + x2 * (-15.0 / 336.0 + x2 * (105.0 / 3456.0))))
    return jnp.sqrt(eps) * series


def waves_kernel(kx_hbm, kz_hbm, o_ref, kx_ref, kz_ref, sems):
    copies = [
        pltpu.make_async_copy(kx_hbm, kx_ref, sems.at[0]),
        pltpu.make_async_copy(kz_hbm, kz_ref, sems.at[1]),
    ]
    for copy in copies:
        copy.start()
    for copy in copies:
        copy.wait()
    iz = lax.axis_index("kz")
    part = 2 * lax.div(iz, 16) + lax.rem(iz, 2)
    lane = lax.broadcasted_iota(jnp.int32, (2, 128), 1)
    kx = jnp.zeros((2, 128), jnp.int32)
    kz = jnp.zeros((2, 128), jnp.int32)
    for r in range(4):
        kx = jnp.where(lax.rem(lane, 4) == r, kx_ref[4 * part + r], kx)
    for r in range(8):
        kz = jnp.where(lax.rem(lane, 8) == r, kz_ref[r], kz)
    rows = jnp.where(lax.broadcasted_iota(jnp.int32, (2, 128), 0) == 0, kz, kx).astype(F32)
    for j in range(o_ref.shape[0]):
        o_ref[j] = rows


def moments_kernel(w_ref, x_ref, r_ref, up_ref, mid_ref, q_ref, qo_ref, ratio_ref, x_own, stage, sems):
    core, _, _ = position()
    ty, tx = wave_group()
    chunks = sems.shape[0]
    per = GRP // chunks

    def copy(g, half):
        rows = pl.ds(8 * per * g, 8 * per)
        return pltpu.make_async_copy(
            x_ref.at[:, :, rows, pl.ds(128 * half, 128)], x_own.at[:, :, rows, :], sems.at[g]
        )

    for half in range(2):
        @pl.when(core == half)
        def _():
            for g in range(chunks):
                copy(g, half).start()

    lane = lax.broadcasted_iota(jnp.int32, (8, 128), 1)
    sub = lax.broadcasted_iota(jnp.int32, (8, 128), 0)
    places = [wave_member(j, ty, tx) for j in range(32)]

    def kz_row(half):
        acc = [jnp.zeros((1, 128), F32) for _ in range(4)]
        for j in range(32):
            acc[j % 4] = jnp.where(lane[0:1] // 8 == places[j] - GRP * half, w_ref[j, 0:1, :], acc[j % 4])
        row = (acc[0] + acc[1]) + (acc[2] + acc[3])
        return (BETA_Z * jnp.broadcast_to(row, (8, 128))) ** 2

    def kx_column(i):
        rows = jnp.where(sub < 4, w_ref[2 * i, 1:2, :], w_ref[2 * i + 1, 1:2, :])
        column = jnp.sum(jnp.where(lane == lax.rem(sub, 4), rows, 0.0), axis=1, keepdims=True)
        return (ALPHA_X * jnp.broadcast_to(column, (8, 128))) ** 2

    kz_own = kz_row(core)
    kz_oth = kz_row(1 - core)
    for i in range(GRP):
        kx = kx_column(i)
        q_ref[8 * i : 8 * i + 8, :] = kx + kz_own
        qo_ref[8 * i : 8 * i + 8, :] = kx + kz_oth

    def tiles(g, first, second):
        @pl.loop(per * g, per * (g + 1), unroll=2)
        def _(i):
            rows = pl.ds(pl.multiple_of(8 * i, 8), 8)
            q = q_ref[rows, :]
            ps = chain(H2 * (q + SHIFT), BLK)
            pq = chain(H2 * q, BLK)
            ratio = ps[PTS] / ps[BLK]
            ratio_ref[rows, :] = ratio
            def put(n, value):
                stage[pl.ds(8 * NUM * i + n, 8, stride=NUM), :] = KAPPA * value

            for c in range(4):
                f = [first(m, c, rows) for m in range(PTS)] + [second(m, c, rows) for m in range(PTS)]
                own = ps[BLK] * f[0]
                nxt = jnp.zeros_like(own)
                mid = jnp.zeros_like(own)
                for m in range(1, BLK):
                    to_own = ps[BLK - m] * f[m]
                    to_nxt = ps[m] * f[m]
                    own = own + to_own
                    nxt = nxt + to_nxt
                    mid = mid + (to_nxt if m <= PTS else to_own)
                put(c, own)
                put(4 + c, nxt)
                mid_ref[i, c] = ratio * (KAPPA * mid)
                if c < 2:
                    own = pq[BLK] * f[0]
                    nxt = pq[1] * f[1]
                    for m in range(1, BLK):
                        own = own + pq[BLK - m] * f[m]
                    for m in range(2, BLK):
                        nxt = nxt + pq[m] * f[m]
                    put(8 + c, own)
                    put(10 + c, nxt)

    for g in range(chunks):
        copy(g, 0).wait()

        @pl.when(core == 0)
        def _():
            tiles(g, lambda m, c, rows: x_own[m, c, rows, :], lambda m, c, rows: r_ref[m, c, rows, :128])

        @pl.when(core != 0)
        def _():
            tiles(g, lambda m, c, rows: r_ref[m, c, rows, 128:], lambda m, c, rows: x_own[m, c, rows, :])

    @pl.loop(0, 64, unroll=4)
    def _(i):
        for k in range(3):
            value = stage[pl.ds(pl.multiple_of(24 * i + 8 * k, 8), 8), :]
            for half in range(2):
                j, a = divmod(2 * k + half, 3)
                up_ref[2 * i + j, a] = value[4 * half : 4 * half + 4, :]


def solve_kernel(m_ref, q_ref, o_ref):
    _, group, chip = position()
    shape = (4, 128)
    q = jnp.broadcast_to(q_ref[pl.ds(GRP * group + chip, 1), :], shape)
    sub = lax.broadcasted_iota(jnp.int32, shape, 0)
    es = H2 * (q + SHIFT)
    eq = H2 * q
    ts = angle(es)
    tq = angle(eq)
    rho = jnp.exp(-BLK * ts)
    rho_seg = jnp.exp(-(BLK * GRP) * ts)
    rho_q = jnp.exp(-BLK * tq)
    rho_q_seg = jnp.exp(-(BLK * GRP) * tq)
    sinh_s = jnp.sqrt(es * (1.0 + 0.25 * es))
    sinh_q = jnp.sqrt(eq * (1.0 + 0.25 * eq))
    scale = 0.5 / (sinh_s * chain(es, BLK)[BLK])
    end_s = jnp.exp(-N * ts)
    inv_s = 1.0 / (1.0 - end_s * end_s)
    end_q = jnp.exp(-N * tq)
    positive = q > 0.0
    inv_q = 1.0 / jnp.where(positive, 1.0 - end_q * end_q, 1.0)
    coth_s = sinh_s * (1.0 + end_s * end_s) * inv_s
    csch_s = 2.0 * sinh_s * end_s * inv_s
    coth_q = jnp.where(positive, sinh_q * (1.0 + end_q * end_q) * inv_q, 1.0 / N)
    csch_q = jnp.where(positive, 2.0 * sinh_q * end_q * inv_q, 1.0 / N)
    m_same = (2.0 - es) * coth_s - (2.0 - eq) * coth_q + 0.5 * (es * es - eq * eq)
    m_cross = (2.0 - eq) * csch_q - (2.0 - es) * csch_s
    inv_det = 1.0 / (m_same * m_same - m_cross * m_cross)
    inv_pq = 1.0 / chain(eq, BLK)[BLK]

    segments = CHIPS // GRP
    ends, heads, falls, rises, firsts = [], [], [], [], []
    for k in range(segments):
        t = []
        for d in range(GRP * k, GRP * (k + 1)):
            value = m_ref[d, 0]
            t.append(value + m_ref[d - 1, 1] if d else value)
        ahead = [t[0]]
        for v in t[1:]:
            ahead.append(rho * ahead[-1] + v)
        ends.append(ahead[-1])
        back = t[-1]
        o_ref[GRP * k + GRP - 1, 0:4, :] = scale * ahead[-1]
        for i in range(GRP - 2, -1, -1):
            o_ref[GRP * k + i, 0:4, :] = scale * (ahead[i] + rho * back)
            back = t[i] + rho * back
        heads.append(back)
        w = [m_ref[d, 2] for d in range(GRP * k, GRP * (k + 1))]
        rise = w[0]
        first = (GRP * k) * w[0]
        for i in range(1, GRP):
            rise = rho_q * rise + w[i]
            first = first + (GRP * k + i) * w[i]
        fall = w[-1]
        for i in range(GRP - 2, -1, -1):
            fall = w[i] + rho_q * fall
        falls.append(fall)
        rises.append(rise)
        firsts.append(first)

    last = m_ref[CHIPS - 1, 1]
    from_lo = [jnp.zeros(shape, F32)]
    for k in range(segments):
        from_lo.append(ends[k] + rho_seg * from_lo[-1])
    at_hi = rho * from_lo[segments] + last
    from_hi = [None] * segments
    value = last
    for k in range(segments - 1, -1, -1):
        from_hi[k] = value
        value = heads[k] + rho_seg * value
    at_lo = value
    fall, rise, first = falls[-1], rises[0], firsts[0]
    for k in range(1, segments):
        fall = falls[segments - 1 - k] + rho_q_seg * fall
        rise = rises[k] + rho_q_seg * rise
        first = first + firsts[k]

    place = jnp.where(sub < 2, 1.0, BLK + 1.0)
    lower = jnp.exp(-place * tq) * fall
    upper = jnp.where(sub < 2, rho_q, 1.0) * rise
    y_hi = jnp.where(positive, (upper - end_q * lower) * inv_q, (BLK * first + place * fall) * (1.0 / N))
    y_lo = lower - end_q * y_hi

    def both(value):
        return jnp.concatenate([value[0:2] + value[2:4], jnp.zeros((2, 128), F32)], axis=0)

    x_lo = scale * jnp.exp(-ts) * at_lo
    x_hi = scale * at_hi
    alpha = (end_s * x_hi - x_lo) * inv_s
    beta = (end_s * x_lo - x_hi) * inv_s
    phi_lo = 2.0 * sinh_s * (x_lo + end_s * beta)
    phi_hi = 2.0 * sinh_s * (x_hi + end_s * alpha)
    w_lo = (2.0 - es) * phi_lo - (2.0 - eq) * (both(y_lo) * inv_pq)
    w_hi = (2.0 - es) * phi_hi - (2.0 - eq) * (both(y_hi) * inv_pq)
    wall_lo = jnp.where(sub < 2, (m_same * w_lo - m_cross * w_hi) * inv_det, 0.0) - x_lo
    wall_hi = jnp.where(sub < 2, (m_same * w_hi - m_cross * w_lo) * inv_det, 0.0) - x_hi
    alpha = (wall_lo - end_s * wall_hi) * inv_s
    beta = (wall_hi - end_s * wall_lo) * inv_s

    power = [None, rho]
    for _ in range(GRP - 1):
        power.append(power[-1] * rho)
    for k in range(segments):
        up = scale * from_lo[k] + alpha * jnp.exp((BLK - 1.0 - BLK * GRP * k) * ts)
        down = scale * from_hi[k] + beta * jnp.exp((BLK * GRP * (k + 1.0) - NY) * ts)
        for i in range(GRP):
            d = GRP * k + i
            value = o_ref[d, 0:4, :] + power[i + 1] * up + power[GRP - i] * down
            o_ref[d, 0:4, :] = value
            if d:
                o_ref[d - 1, 4:8, :] = value
    o_ref[CHIPS - 1, 4:8, :] = x_hi + alpha * end_s + beta


def middle_kernel(b_ref, mid_ref, ratio_ref, own_ref, send_ref):
    core, _, _ = position()

    def tiles(lower, upper):
        @pl.loop(0, GRP, unroll=2)
        def _(i):
            ratio = ratio_ref[pl.ds(pl.multiple_of(8 * i, 8), 8), :]
            for c in range(4):
                a = b_ref[pl.ds(64 * i + c, 8, stride=8), :]
                b = b_ref[pl.ds(64 * i + 4 + c, 8, stride=8), :]
                x = ratio * (a + b) + mid_ref[i, c]
                lower[i, c] = a
                lower[i, 4 + c] = x
                upper[i, c] = x
                upper[i, 4 + c] = b

    @pl.when(core == 0)
    def _():
        tiles(own_ref, send_ref)

    @pl.when(core != 0)
    def _():
        tiles(send_ref, own_ref)


def points_kernel(other, x_ref, ends, q_ref, *refs):
    o_ref, buf, sems = refs[-3:]
    core, _, _ = position()
    chunks = sems.shape[0]
    per = GRP // chunks

    def tile(i, lanes):
        rows = pl.ds(pl.multiple_of(8 * i, 8), 8)
        ps = chain(H2 * (q_ref[rows, :] + SHIFT), PTS)
        ratio = [None] + [ps[m] / ps[m + 1] for m in range(1, PTS)]
        for c in range(4):
            a = ends[i, c]
            y = [None, KAPPA * x_ref[1, c, rows, lanes] + a]
            for m in range(2, PTS):
                y.append(KAPPA * x_ref[m, c, rows, lanes] + ratio[m - 1] * y[-1])
            buf[0, c, rows, :] = a
            value = ends[i, 4 + c]
            for m in range(PTS - 1, 0, -1):
                value = ratio[m] * (y[m] + value)
                buf[m, c, rows, :] = value

    def copy(g, half):
        rows = pl.ds(8 * per * g, 8 * per)
        return pltpu.make_async_copy(
            buf.at[:, :, rows, :], o_ref.at[:, :, rows, pl.ds(128 * half, 128)], sems.at[g]
        )

    for half in range(2):
        @pl.when(core == (1 - half if other else half))
        def _():
            for g in range(chunks):
                @pl.loop(per * g, per * (g + 1), unroll=2)
                def _(i):
                    tile(i, slice(128 * half, 128 * half + 128))

                copy(g, half).start()

    for g in range(chunks):
        copy(g, 0).wait()


def in_vmem(value):
    return pltpu.with_memory_space_constraint(value, pltpu.VMEM)


def local_call(kernel, operands, shapes):
    return pl.pallas_call(
        kernel,
        in_specs=[pl.BlockSpec(memory_space=pltpu.VMEM)] * len(operands),
        out_specs=[pl.BlockSpec(memory_space=pltpu.VMEM)] * len(shapes),
        out_shape=[pltpu.VMEM(shape, F32) for shape in shapes],
        compiler_params=pltpu.CompilerParams(vmem_limit_bytes=8 << 20),
    )(*[in_vmem(v) for v in operands])


def on_device(forcing, kx_wave, kz_wave):
    both = ("kx", "kz")
    wave_groups = [
        [32 * (j // 4) + wave_member(j, ty, tx) for j in range(32)] for ty in range(4) for tx in range(2)
    ]
    core_groups = [[2 * k + c for k in range(CHIPS)] for c in range(2)]
    pairs = [(i, i ^ 1) for i in range(32)]

    vmem = pl.BlockSpec(memory_space=pltpu.VMEM)
    hbm = pl.BlockSpec(memory_space=pltpu.HBM)
    params = pltpu.CompilerParams(vmem_limit_bytes=8 << 20)
    half_shape = (PTS, 4, 128, 128)

    swapped = lax.ppermute(forcing, "kz", pairs)

    payload = pl.pallas_call(
        waves_kernel,
        in_specs=[hbm] * 2,
        out_specs=vmem,
        out_shape=pltpu.VMEM((32, 2, 128), F32),
        scratch_shapes=[
            pltpu.SMEM(kx_wave.shape, jnp.int32),
            pltpu.SMEM(kz_wave.shape, jnp.int32),
            pltpu.SemaphoreType.DMA((2,)),
        ],
        compiler_params=params,
    )(*[pltpu.with_memory_space_constraint(v, pltpu.HBM) for v in (kx_wave, kz_wave)])
    waves = lax.all_to_all(payload, both, 0, 0, tiled=True, axis_index_groups=wave_groups)
    up, mid, q_own, q_oth, ratio = pl.pallas_call(
        moments_kernel,
        in_specs=[vmem, hbm, vmem],
        out_specs=[vmem] * 5,
        out_shape=[
            pltpu.VMEM(shape, F32)
            for shape in ((CHIPS, 3, 4, 128), (GRP, 4, 8, 128), (128, 128), (128, 128), (128, 128))
        ],
        scratch_shapes=[
            pltpu.VMEM(half_shape, F32),
            pltpu.VMEM((NUM * CHIPS, 128), F32),
            pltpu.SemaphoreType.DMA((4,)),
        ],
        compiler_params=params,
    )(in_vmem(waves), pltpu.with_memory_space_constraint(forcing, pltpu.HBM), in_vmem(swapped))
    blocks = lax.all_to_all(up, both, 0, 0, tiled=True, axis_index_groups=core_groups)
    (ends,) = local_call(solve_kernel, (blocks, q_own), ((CHIPS, 8, 128),))
    ends = lax.all_to_all(ends, both, 0, 0, tiled=True, axis_index_groups=core_groups)
    ends = ends.reshape(8 * CHIPS, 128)
    own, send = local_call(middle_kernel, (ends, mid, ratio), ((GRP, 8, 8, 128),) * 2)
    received = lax.ppermute(send, "kz", pairs)

    def points(other, operands, *made):
        return pl.pallas_call(
            functools.partial(points_kernel, other),
            in_specs=[vmem] * 3 + [hbm] * len(made),
            out_specs=hbm,
            out_shape=pltpu.HBM(forcing.shape, F32),
            input_output_aliases={3: 0} if made else {},
            scratch_shapes=[pltpu.VMEM(half_shape, F32), pltpu.SemaphoreType.DMA((4,))],
            compiler_params=params,
            cost_estimate=pl.CostEstimate(flops=8 << 20, bytes_accessed=4 << 20, transcendentals=0),
        )(*[in_vmem(v) for v in operands], *made)

    fields = points(False, (forcing, own, q_own))
    return points(True, (forcing, received, q_oth), fields)


def solution(mesh):
    placed = (P(("kx", "kz"), None, None, None), P("kx"), P("kz"))
    return jax.shard_map(
        on_device,
        mesh=mesh,
        in_specs=placed,
        out_specs=P(("kx", "kz"), None, None, None),
        check_vma=False,
    )
```

```python
import functools

import jax
import jax.numpy as jnp
from jax import lax
from jax.experimental import pallas as pl
from jax.experimental.pallas import tpu as pltpu
from jax.sharding import PartitionSpec as P

NY = 1536
N = NY + 1
H2 = (2.0 / N) ** 2
SHIFT = 4000.0
KAPPA = SHIFT * H2
ALPHA_X = 0.25
BETA_Z = 2.0 / 3.0
PTS = 6
BLK = 12
GRP = 16
CHIPS = 128
NUM = 12
F32 = jnp.float32


def position():
    iz = lax.axis_index("kz")
    return lax.rem(iz, 2), lax.axis_index("kx"), lax.div(iz, 2)


def wave_group():
    ix = lax.axis_index("kx")
    iz = lax.axis_index("kz")
    x_lo, y = lax.div(ix, 4), lax.rem(ix, 4)
    z, x_hi = lax.div(iz, 4), lax.rem(lax.div(iz, 2), 2)
    return lax.rem(y - z + 8, 4), lax.rem(x_lo + x_hi + lax.div(z, 4), 2)


def wave_member(j, ty, tx):
    x_lo, y, b, core = j // 16, j // 4 % 4, j // 2 % 2, j % 2
    return 4 * ((y - ty + 4) % 4 + 4 * b) + 2 * ((x_lo + tx + b) % 2) + core


def chain(eps, n):
    p = [None, jnp.ones_like(eps)]
    diff = 1.0 + eps
    for _ in range(2, n + 1):
        p.append(p[-1] + diff)
        diff = diff + eps * p[-1]
    return p


def angle(eps):
    x2 = 0.25 * eps
    series = 1.0 + x2 * (-1.0 / 6.0 + x2 * (3.0 / 40.0 + x2 * (-15.0 / 336.0 + x2 * (105.0 / 3456.0))))
    return jnp.sqrt(eps) * series


def waves_kernel(kx_hbm, kz_hbm, o_ref, kx_ref, kz_ref, sems):
    copies = [
        pltpu.make_async_copy(kx_hbm, kx_ref, sems.at[0]),
        pltpu.make_async_copy(kz_hbm, kz_ref, sems.at[1]),
    ]
    for copy in copies:
        copy.start()
    for copy in copies:
        copy.wait()
    iz = lax.axis_index("kz")
    part = 2 * lax.div(iz, 16) + lax.rem(iz, 2)
    lane = lax.broadcasted_iota(jnp.int32, (2, 128), 1)
    kx = jnp.zeros((2, 128), jnp.int32)
    kz = jnp.zeros((2, 128), jnp.int32)
    for r in range(4):
        kx = jnp.where(lax.rem(lane, 4) == r, kx_ref[4 * part + r], kx)
    for r in range(8):
        kz = jnp.where(lax.rem(lane, 8) == r, kz_ref[r], kz)
    rows = jnp.where(lax.broadcasted_iota(jnp.int32, (2, 128), 0) == 0, kz, kx).astype(F32)
    for j in range(o_ref.shape[0]):
        o_ref[j] = rows


def moments_kernel(w_ref, x_ref, r_ref, turn_ref, up_ref, mid_ref, q_ref, qo_ref, ratio_ref, x_own, stage, sems):
    core, _, _ = position()
    ty, tx = wave_group()
    chunks = sems.shape[0]
    per = GRP // chunks

    def copy(g, half):
        rows = pl.ds(8 * per * g, 8 * per)
        return pltpu.make_async_copy(
            x_ref.at[:, :, rows, pl.ds(128 * half, 128)], x_own.at[:, :, rows, :], sems.at[g]
        )

    for half in range(2):
        @pl.when(core == half)
        def _():
            for g in range(chunks):
                copy(g, half).start()

    lane = lax.broadcasted_iota(jnp.int32, (8, 128), 1)
    sub = lax.broadcasted_iota(jnp.int32, (8, 128), 0)
    places = [wave_member(j, ty, tx) for j in range(32)]

    def kz_row(half):
        acc = [jnp.zeros((1, 128), F32) for _ in range(4)]
        for j in range(32):
            acc[j % 4] = jnp.where(lane[0:1] // 8 == places[j] - GRP * half, w_ref[j, 0:1, :], acc[j % 4])
        row = (acc[0] + acc[1]) + (acc[2] + acc[3])
        return (BETA_Z * jnp.broadcast_to(row, (8, 128))) ** 2

    def kx_column(i):
        rows = jnp.where(sub < 4, w_ref[2 * i, 1:2, :], w_ref[2 * i + 1, 1:2, :])
        column = jnp.sum(jnp.where(lane == lax.rem(sub, 4), rows, 0.0), axis=1, keepdims=True)
        return (ALPHA_X * jnp.broadcast_to(column, (8, 128))) ** 2

    kz_own = kz_row(core)
    kz_oth = kz_row(1 - core)
    for i in range(GRP):
        kx = kx_column(i)
        q_ref[8 * i : 8 * i + 8, :] = kx + kz_own
        qo_ref[8 * i : 8 * i + 8, :] = kx + kz_oth

    def tiles(g, first, second):
        @pl.loop(per * g, per * (g + 1), unroll=2)
        def _(i):
            rows = pl.ds(pl.multiple_of(8 * i, 8), 8)
            q = q_ref[rows, :]
            ps = chain(H2 * (q + SHIFT), BLK)
            pq = chain(H2 * q, BLK)
            ratio = ps[PTS] / ps[BLK]
            ratio_ref[rows, :] = ratio
            def put(n, value):
                stage[pl.ds(8 * NUM * i + n, 8, stride=NUM), :] = KAPPA * value

            for c in range(4):
                f = [first(m, c, rows) for m in range(PTS)] + [second(m, c, rows) for m in range(PTS)]
                own = ps[BLK] * f[0]
                nxt = jnp.zeros_like(own)
                mid = jnp.zeros_like(own)
                for m in range(1, BLK):
                    to_own = ps[BLK - m] * f[m]
                    to_nxt = ps[m] * f[m]
                    own = own + to_own
                    nxt = nxt + to_nxt
                    mid = mid + (to_nxt if m <= PTS else to_own)
                put(c, own)
                put(4 + c, nxt)
                mid_ref[i, c] = ratio * (KAPPA * mid)
                if c < 2:
                    own = pq[BLK] * f[0]
                    nxt = pq[1] * f[1]
                    for m in range(1, BLK):
                        own = own + pq[BLK - m] * f[m]
                    for m in range(2, BLK):
                        nxt = nxt + pq[m] * f[m]
                    put(8 + c, own)
                    put(10 + c, nxt)

    for g in range(chunks):
        copy(g, 0).wait()

        @pl.when(core == 0)
        def _():
            tiles(g, lambda m, c, rows: x_own[m, c, rows, :], lambda m, c, rows: r_ref[m, c, rows, :128])

        @pl.when(core != 0)
        def _():
            tiles(g, lambda m, c, rows: r_ref[m, c, rows, 128:], lambda m, c, rows: x_own[m, c, rows, :])

    @pl.loop(0, 64, unroll=4)
    def _(i):
        for k in range(3):
            value = stage[pl.ds(pl.multiple_of(24 * i + 8 * k, 8), 8), :]
            for half in range(2):
                j, a = divmod(2 * k + half, 3)
                up_ref[2 * i + j, a] = value[4 * half : 4 * half + 4, :]


def solve_kernel(m_ref, q_ref, o_ref):
    _, group, chip = position()
    shape = (4, 128)
    q = jnp.broadcast_to(q_ref[pl.ds(GRP * group + chip, 1), :], shape)
    sub = lax.broadcasted_iota(jnp.int32, shape, 0)
    es = H2 * (q + SHIFT)
    eq = H2 * q
    ts = angle(es)
    tq = angle(eq)
    rho = jnp.exp(-BLK * ts)
    rho_seg = jnp.exp(-(BLK * GRP) * ts)
    rho_q = jnp.exp(-BLK * tq)
    rho_q_seg = jnp.exp(-(BLK * GRP) * tq)
    sinh_s = jnp.sqrt(es * (1.0 + 0.25 * es))
    sinh_q = jnp.sqrt(eq * (1.0 + 0.25 * eq))
    scale = 0.5 / (sinh_s * chain(es, BLK)[BLK])
    end_s = jnp.exp(-N * ts)
    inv_s = 1.0 / (1.0 - end_s * end_s)
    end_q = jnp.exp(-N * tq)
    positive = q > 0.0
    inv_q = 1.0 / jnp.where(positive, 1.0 - end_q * end_q, 1.0)
    coth_s = sinh_s * (1.0 + end_s * end_s) * inv_s
    csch_s = 2.0 * sinh_s * end_s * inv_s
    coth_q = jnp.where(positive, sinh_q * (1.0 + end_q * end_q) * inv_q, 1.0 / N)
    csch_q = jnp.where(positive, 2.0 * sinh_q * end_q * inv_q, 1.0 / N)
    m_same = (2.0 - es) * coth_s - (2.0 - eq) * coth_q + 0.5 * (es * es - eq * eq)
    m_cross = (2.0 - eq) * csch_q - (2.0 - es) * csch_s
    inv_det = 1.0 / (m_same * m_same - m_cross * m_cross)
    inv_pq = 1.0 / chain(eq, BLK)[BLK]

    segments = CHIPS // GRP
    ends, heads, falls, rises, firsts = [], [], [], [], []
    for k in range(segments):
        t = []
        for d in range(GRP * k, GRP * (k + 1)):
            value = m_ref[d, 0]
            t.append(value + m_ref[d - 1, 1] if d else value)
        ahead = [t[0]]
        for v in t[1:]:
            ahead.append(rho * ahead[-1] + v)
        ends.append(ahead[-1])
        back = t[-1]
        o_ref[GRP * k + GRP - 1, 0:4, :] = scale * ahead[-1]
        for i in range(GRP - 2, -1, -1):
            o_ref[GRP * k + i, 0:4, :] = scale * (ahead[i] + rho * back)
            back = t[i] + rho * back
        heads.append(back)
        w = [m_ref[d, 2] for d in range(GRP * k, GRP * (k + 1))]
        rise = w[0]
        first = (GRP * k) * w[0]
        for i in range(1, GRP):
            rise = rho_q * rise + w[i]
            first = first + (GRP * k + i) * w[i]
        fall = w[-1]
        for i in range(GRP - 2, -1, -1):
            fall = w[i] + rho_q * fall
        falls.append(fall)
        rises.append(rise)
        firsts.append(first)

    last = m_ref[CHIPS - 1, 1]
    from_lo = [jnp.zeros(shape, F32)]
    for k in range(segments):
        from_lo.append(ends[k] + rho_seg * from_lo[-1])
    at_hi = rho * from_lo[segments] + last
    from_hi = [None] * segments
    value = last
    for k in range(segments - 1, -1, -1):
        from_hi[k] = value
        value = heads[k] + rho_seg * value
    at_lo = value
    fall, rise, first = falls[-1], rises[0], firsts[0]
    for k in range(1, segments):
        fall = falls[segments - 1 - k] + rho_q_seg * fall
        rise = rises[k] + rho_q_seg * rise
        first = first + firsts[k]

    place = jnp.where(sub < 2, 1.0, BLK + 1.0)
    lower = jnp.exp(-place * tq) * fall
    upper = jnp.where(sub < 2, rho_q, 1.0) * rise
    y_hi = jnp.where(positive, (upper - end_q * lower) * inv_q, (BLK * first + place * fall) * (1.0 / N))
    y_lo = lower - end_q * y_hi

    def both(value):
        return jnp.concatenate([value[0:2] + value[2:4], jnp.zeros((2, 128), F32)], axis=0)

    x_lo = scale * jnp.exp(-ts) * at_lo
    x_hi = scale * at_hi
    alpha = (end_s * x_hi - x_lo) * inv_s
    beta = (end_s * x_lo - x_hi) * inv_s
    phi_lo = 2.0 * sinh_s * (x_lo + end_s * beta)
    phi_hi = 2.0 * sinh_s * (x_hi + end_s * alpha)
    w_lo = (2.0 - es) * phi_lo - (2.0 - eq) * (both(y_lo) * inv_pq)
    w_hi = (2.0 - es) * phi_hi - (2.0 - eq) * (both(y_hi) * inv_pq)
    wall_lo = jnp.where(sub < 2, (m_same * w_lo - m_cross * w_hi) * inv_det, 0.0) - x_lo
    wall_hi = jnp.where(sub < 2, (m_same * w_hi - m_cross * w_lo) * inv_det, 0.0) - x_hi
    alpha = (wall_lo - end_s * wall_hi) * inv_s
    beta = (wall_hi - end_s * wall_lo) * inv_s

    power = [None, rho]
    for _ in range(GRP - 1):
        power.append(power[-1] * rho)
    for k in range(segments):
        up = scale * from_lo[k] + alpha * jnp.exp((BLK - 1.0 - BLK * GRP * k) * ts)
        down = scale * from_hi[k] + beta * jnp.exp((BLK * GRP * (k + 1.0) - NY) * ts)
        for i in range(GRP):
            d = GRP * k + i
            value = o_ref[d, 0:4, :] + power[i + 1] * up + power[GRP - i] * down
            o_ref[d, 0:4, :] = value
            if d:
                o_ref[d - 1, 4:8, :] = value
    o_ref[CHIPS - 1, 4:8, :] = x_hi + alpha * end_s + beta


def middle_kernel(b_ref, mid_ref, ratio_ref, own_ref, send_ref):
    core, _, _ = position()

    def tiles(lower, upper):
        @pl.loop(0, GRP, unroll=2)
        def _(i):
            ratio = ratio_ref[pl.ds(pl.multiple_of(8 * i, 8), 8), :]
            for c in range(4):
                a = b_ref[pl.ds(64 * i + c, 8, stride=8), :]
                b = b_ref[pl.ds(64 * i + 4 + c, 8, stride=8), :]
                x = ratio * (a + b) + mid_ref[i, c]
                lower[i, c] = a
                lower[i, 4 + c] = x
                upper[i, c] = x
                upper[i, 4 + c] = b

    @pl.when(core == 0)
    def _():
        tiles(own_ref, send_ref)

    @pl.when(core != 0)
    def _():
        tiles(send_ref, own_ref)


def points_kernel(other, x_ref, ends, q_ref, *refs):
    o_ref, buf, sems = refs[-3:]
    core, _, _ = position()
    chunks = sems.shape[0]
    per = GRP // chunks

    def tile(i, lanes):
        rows = pl.ds(pl.multiple_of(8 * i, 8), 8)
        ps = chain(H2 * (q_ref[rows, :] + SHIFT), PTS)
        ratio = [None] + [ps[m] / ps[m + 1] for m in range(1, PTS)]
        for c in range(4):
            a = ends[i, c]
            y = [None, KAPPA * x_ref[1, c, rows, lanes] + a]
            for m in range(2, PTS):
                y.append(KAPPA * x_ref[m, c, rows, lanes] + ratio[m - 1] * y[-1])
            buf[0, c, rows, :] = a
            value = ends[i, 4 + c]
            for m in range(PTS - 1, 0, -1):
                value = ratio[m] * (y[m] + value)
                buf[m, c, rows, :] = value

    def copy(g, half):
        rows = pl.ds(8 * per * g, 8 * per)
        return pltpu.make_async_copy(
            buf.at[:, :, rows, :], o_ref.at[:, :, rows, pl.ds(128 * half, 128)], sems.at[g]
        )

    for half in range(2):
        @pl.when(core == (1 - half if other else half))
        def _():
            for g in range(chunks):
                @pl.loop(per * g, per * (g + 1), unroll=2)
                def _(i):
                    tile(i, slice(128 * half, 128 * half + 128))

                copy(g, half).start()

    for g in range(chunks):
        copy(g, 0).wait()


def in_vmem(value):
    return pltpu.with_memory_space_constraint(value, pltpu.VMEM)


def local_call(kernel, operands, shapes):
    return pl.pallas_call(
        kernel,
        in_specs=[pl.BlockSpec(memory_space=pltpu.VMEM)] * len(operands),
        out_specs=[pl.BlockSpec(memory_space=pltpu.VMEM)] * len(shapes),
        out_shape=[pltpu.VMEM(shape, F32) for shape in shapes],
        compiler_params=pltpu.CompilerParams(vmem_limit_bytes=8 << 20),
    )(*[in_vmem(v) for v in operands])


def on_device(forcing, kx_wave, kz_wave):
    both = ("kx", "kz")
    wave_groups = [
        [32 * (j // 4) + wave_member(j, ty, tx) for j in range(32)] for ty in range(4) for tx in range(2)
    ]
    core_groups = [[2 * k + c for k in range(CHIPS)] for c in range(2)]
    pairs = [(i, i ^ 1) for i in range(32)]

    vmem = pl.BlockSpec(memory_space=pltpu.VMEM)
    hbm = pl.BlockSpec(memory_space=pltpu.HBM)
    params = pltpu.CompilerParams(vmem_limit_bytes=8 << 20)
    half_shape = (PTS, 4, 128, 128)

    swapped = lax.ppermute(forcing, "kz", pairs)

    payload = pl.pallas_call(
        waves_kernel,
        in_specs=[hbm] * 2,
        out_specs=vmem,
        out_shape=pltpu.VMEM((32, 2, 128), F32),
        scratch_shapes=[
            pltpu.SMEM(kx_wave.shape, jnp.int32),
            pltpu.SMEM(kz_wave.shape, jnp.int32),
            pltpu.SemaphoreType.DMA((2,)),
        ],
        compiler_params=params,
    )(*[pltpu.with_memory_space_constraint(v, pltpu.HBM) for v in (kx_wave, kz_wave)])
    waves = lax.all_to_all(payload, both, 0, 0, tiled=True, axis_index_groups=wave_groups)
    turn = lax.ppermute(waves, "kz", [(i, i ^ 2) for i in range(0, 32, 2)])

    up, mid, q_own, q_oth, ratio = pl.pallas_call(
        moments_kernel,
        in_specs=[vmem, hbm, vmem, vmem],
        out_specs=[vmem] * 5,
        out_shape=[
            pltpu.VMEM(shape, F32)
            for shape in ((CHIPS, 3, 4, 128), (GRP, 4, 8, 128), (128, 128), (128, 128), (128, 128))
        ],
        scratch_shapes=[
            pltpu.VMEM(half_shape, F32),
            pltpu.VMEM((NUM * CHIPS, 128), F32),
            pltpu.SemaphoreType.DMA((4,)),
        ],
        compiler_params=params,
    )(in_vmem(waves), pltpu.with_memory_space_constraint(forcing, pltpu.HBM), in_vmem(swapped), in_vmem(turn))
    blocks = lax.all_to_all(up, both, 0, 0, tiled=True, axis_index_groups=core_groups)
    (ends,) = local_call(solve_kernel, (blocks, q_own), ((CHIPS, 8, 128),))
    ends = lax.all_to_all(ends, both, 0, 0, tiled=True, axis_index_groups=core_groups)
    ends = ends.reshape(8 * CHIPS, 128)
    own, send = local_call(middle_kernel, (ends, mid, ratio), ((GRP, 8, 8, 128),) * 2)
    received = lax.ppermute(send, "kz", pairs)

    def points(other, operands, *made):
        return pl.pallas_call(
            functools.partial(points_kernel, other),
            in_specs=[vmem] * 3 + [hbm] * len(made),
            out_specs=hbm,
            out_shape=pltpu.HBM(forcing.shape, F32),
            input_output_aliases={3: 0} if made else {},
            scratch_shapes=[pltpu.VMEM(half_shape, F32), pltpu.SemaphoreType.DMA((4,))],
            compiler_params=params,
            cost_estimate=pl.CostEstimate(flops=8 << 20, bytes_accessed=4 << 20, transcendentals=0),
        )(*[in_vmem(v) for v in operands], *made)

    fields = points(False, (forcing, own, q_own))
    return points(True, (forcing, received, q_oth), fields)


def solution(mesh):
    placed = (P(("kx", "kz"), None, None, None), P("kx"), P("kz"))
    return jax.shard_map(
        on_device,
        mesh=mesh,
        in_specs=placed,
        out_specs=P(("kx", "kz"), None, None, None),
        check_vma=False,
    )
```

```python
import functools

import jax
import jax.numpy as jnp
from jax import lax
from jax.experimental import pallas as pl
from jax.experimental.pallas import tpu as pltpu
from jax.sharding import PartitionSpec as P

NY = 1536
N = NY + 1
H2 = (2.0 / N) ** 2
SHIFT = 4000.0
KAPPA = SHIFT * H2
ALPHA_X = 0.25
BETA_Z = 2.0 / 3.0
PTS = 6
BLK = 12
GRP = 16
CHIPS = 128
NUM = 12
F32 = jnp.float32


def position():
    iz = lax.axis_index("kz")
    return lax.rem(iz, 2), lax.axis_index("kx"), lax.div(iz, 2)


def wave_group():
    ix = lax.axis_index("kx")
    iz = lax.axis_index("kz")
    x_lo, y = lax.div(ix, 4), lax.rem(ix, 4)
    z, x_hi = lax.div(iz, 4), lax.rem(lax.div(iz, 2), 2)
    return lax.rem(y - z + 8, 4), lax.rem(x_lo + x_hi, 2)


def wave_member(j, ty, tx):
    x_lo, y, b, core = j // 16, j // 4 % 4, j // 2 % 2, j % 2
    return 4 * ((y - ty + 4) % 4 + 4 * b) + 2 * ((x_lo + tx) % 2) + core


def chain(eps, n):
    p = [None, jnp.ones_like(eps)]
    diff = 1.0 + eps
    for _ in range(2, n + 1):
        p.append(p[-1] + diff)
        diff = diff + eps * p[-1]
    return p


def angle(eps):
    x2 = 0.25 * eps
    series = 1.0 + x2 * (-1.0 / 6.0 + x2 * (3.0 / 40.0 + x2 * (-15.0 / 336.0 + x2 * (105.0 / 3456.0))))
    return jnp.sqrt(eps) * series


def waves_kernel(kx_hbm, kz_hbm, o_ref, kx_ref, kz_ref, sems):
    copies = [
        pltpu.make_async_copy(kx_hbm, kx_ref, sems.at[0]),
        pltpu.make_async_copy(kz_hbm, kz_ref, sems.at[1]),
    ]
    for copy in copies:
        copy.start()
    for copy in copies:
        copy.wait()
    iz = lax.axis_index("kz")
    part = 2 * lax.div(iz, 16) + lax.rem(iz, 2)
    lane = lax.broadcasted_iota(jnp.int32, (2, 128), 1)
    kx = jnp.zeros((2, 128), jnp.int32)
    kz = jnp.zeros((2, 128), jnp.int32)
    for r in range(4):
        kx = jnp.where(lax.rem(lane, 4) == r, kx_ref[4 * part + r], kx)
    for r in range(8):
        kz = jnp.where(lax.rem(lane, 8) == r, kz_ref[r], kz)
    rows = jnp.where(lax.broadcasted_iota(jnp.int32, (2, 128), 0) == 0, kz, kx).astype(F32)
    for j in range(o_ref.shape[0]):
        o_ref[j] = rows


def moments_kernel(w_ref, x_ref, r_ref, turn_ref, up_ref, mid_ref, q_ref, qo_ref, ratio_ref, x_own, stage, sems):
    core, _, _ = position()
    ty, tx = wave_group()
    chunks = sems.shape[0]
    per = GRP // chunks

    def copy(g, half):
        rows = pl.ds(8 * per * g, 8 * per)
        return pltpu.make_async_copy(
            x_ref.at[:, :, rows, pl.ds(128 * half, 128)], x_own.at[:, :, rows, :], sems.at[g]
        )

    for half in range(2):
        @pl.when(core == half)
        def _():
            for g in range(chunks):
                copy(g, half).start()

    lane = lax.broadcasted_iota(jnp.int32, (8, 128), 1)
    sub = lax.broadcasted_iota(jnp.int32, (8, 128), 0)
    places = [wave_member(j, ty, tx) for j in range(32)]

    def kz_row(half):
        acc = [jnp.zeros((1, 128), F32) for _ in range(4)]
        for j in range(32):
            acc[j % 4] = jnp.where(lane[0:1] // 8 == places[j] - GRP * half, w_ref[j, 0:1, :], acc[j % 4])
        row = (acc[0] + acc[1]) + (acc[2] + acc[3])
        return (BETA_Z * jnp.broadcast_to(row, (8, 128))) ** 2

    def kx_column(i):
        rows = jnp.where(sub < 4, w_ref[2 * i, 1:2, :], w_ref[2 * i + 1, 1:2, :])
        column = jnp.sum(jnp.where(lane == lax.rem(sub, 4), rows, 0.0), axis=1, keepdims=True)
        return (ALPHA_X * jnp.broadcast_to(column, (8, 128))) ** 2

    kz_own = kz_row(core)
    kz_oth = kz_row(1 - core)
    for i in range(GRP):
        kx = kx_column(i)
        q_ref[8 * i : 8 * i + 8, :] = kx + kz_own
        qo_ref[8 * i : 8 * i + 8, :] = kx + kz_oth

    def tiles(g, first, second):
        @pl.loop(per * g, per * (g + 1), unroll=2)
        def _(i):
            rows = pl.ds(pl.multiple_of(8 * i, 8), 8)
            q = q_ref[rows, :]
            ps = chain(H2 * (q + SHIFT), BLK)
            pq = chain(H2 * q, BLK)
            ratio = ps[PTS] / ps[BLK]
            ratio_ref[rows, :] = ratio
            def put(n, value):
                stage[pl.ds(8 * NUM * i + n, 8, stride=NUM), :] = KAPPA * value

            for c in range(4):
                f = [first(m, c, rows) for m in range(PTS)] + [second(m, c, rows) for m in range(PTS)]
                own = ps[BLK] * f[0]
                nxt = jnp.zeros_like(own)
                mid = jnp.zeros_like(own)
                for m in range(1, BLK):
                    to_own = ps[BLK - m] * f[m]
                    to_nxt = ps[m] * f[m]
                    own = own + to_own
                    nxt = nxt + to_nxt
                    mid = mid + (to_nxt if m <= PTS else to_own)
                put(c, own)
                put(4 + c, nxt)
                mid_ref[i, c] = ratio * (KAPPA * mid)
                if c < 2:
                    own = pq[BLK] * f[0]
                    nxt = pq[1] * f[1]
                    for m in range(1, BLK):
                        own = own + pq[BLK - m] * f[m]
                    for m in range(2, BLK):
                        nxt = nxt + pq[m] * f[m]
                    put(8 + c, own)
                    put(10 + c, nxt)

    for g in range(chunks):
        copy(g, 0).wait()

        @pl.when(core == 0)
        def _():
            tiles(g, lambda m, c, rows: x_own[m, c, rows, :], lambda m, c, rows: r_ref[m, c, rows, :128])

        @pl.when(core != 0)
        def _():
            tiles(g, lambda m, c, rows: r_ref[m, c, rows, 128:], lambda m, c, rows: x_own[m, c, rows, :])

    @pl.loop(0, 64, unroll=4)
    def _(i):
        for k in range(3):
            value = stage[pl.ds(pl.multiple_of(24 * i + 8 * k, 8), 8), :]
            for half in range(2):
                j, a = divmod(2 * k + half, 3)
                up_ref[2 * i + j, a] = value[4 * half : 4 * half + 4, :]


def solve_kernel(m_ref, q_ref, o_ref):
    _, group, chip = position()
    shape = (4, 128)
    q = jnp.broadcast_to(q_ref[pl.ds(GRP * group + chip, 1), :], shape)
    sub = lax.broadcasted_iota(jnp.int32, shape, 0)
    es = H2 * (q + SHIFT)
    eq = H2 * q
    ts = angle(es)
    tq = angle(eq)
    rho = jnp.exp(-BLK * ts)
    rho_seg = jnp.exp(-(BLK * GRP) * ts)
    rho_q = jnp.exp(-BLK * tq)
    rho_q_seg = jnp.exp(-(BLK * GRP) * tq)
    sinh_s = jnp.sqrt(es * (1.0 + 0.25 * es))
    sinh_q = jnp.sqrt(eq * (1.0 + 0.25 * eq))
    scale = 0.5 / (sinh_s * chain(es, BLK)[BLK])
    end_s = jnp.exp(-N * ts)
    inv_s = 1.0 / (1.0 - end_s * end_s)
    end_q = jnp.exp(-N * tq)
    positive = q > 0.0
    inv_q = 1.0 / jnp.where(positive, 1.0 - end_q * end_q, 1.0)
    coth_s = sinh_s * (1.0 + end_s * end_s) * inv_s
    csch_s = 2.0 * sinh_s * end_s * inv_s
    coth_q = jnp.where(positive, sinh_q * (1.0 + end_q * end_q) * inv_q, 1.0 / N)
    csch_q = jnp.where(positive, 2.0 * sinh_q * end_q * inv_q, 1.0 / N)
    m_same = (2.0 - es) * coth_s - (2.0 - eq) * coth_q + 0.5 * (es * es - eq * eq)
    m_cross = (2.0 - eq) * csch_q - (2.0 - es) * csch_s
    inv_det = 1.0 / (m_same * m_same - m_cross * m_cross)
    inv_pq = 1.0 / chain(eq, BLK)[BLK]

    segments = CHIPS // GRP
    ends, heads, falls, rises, firsts = [], [], [], [], []
    for k in range(segments):
        t = []
        for d in range(GRP * k, GRP * (k + 1)):
            value = m_ref[d, 0]
            t.append(value + m_ref[d - 1, 1] if d else value)
        ahead = [t[0]]
        for v in t[1:]:
            ahead.append(rho * ahead[-1] + v)
        ends.append(ahead[-1])
        back = t[-1]
        o_ref[GRP * k + GRP - 1, 0:4, :] = scale * ahead[-1]
        for i in range(GRP - 2, -1, -1):
            o_ref[GRP * k + i, 0:4, :] = scale * (ahead[i] + rho * back)
            back = t[i] + rho * back
        heads.append(back)
        w = [m_ref[d, 2] for d in range(GRP * k, GRP * (k + 1))]
        rise = w[0]
        first = (GRP * k) * w[0]
        for i in range(1, GRP):
            rise = rho_q * rise + w[i]
            first = first + (GRP * k + i) * w[i]
        fall = w[-1]
        for i in range(GRP - 2, -1, -1):
            fall = w[i] + rho_q * fall
        falls.append(fall)
        rises.append(rise)
        firsts.append(first)

    last = m_ref[CHIPS - 1, 1]
    from_lo = [jnp.zeros(shape, F32)]
    for k in range(segments):
        from_lo.append(ends[k] + rho_seg * from_lo[-1])
    at_hi = rho * from_lo[segments] + last
    from_hi = [None] * segments
    value = last
    for k in range(segments - 1, -1, -1):
        from_hi[k] = value
        value = heads[k] + rho_seg * value
    at_lo = value
    fall, rise, first = falls[-1], rises[0], firsts[0]
    for k in range(1, segments):
        fall = falls[segments - 1 - k] + rho_q_seg * fall
        rise = rises[k] + rho_q_seg * rise
        first = first + firsts[k]

    place = jnp.where(sub < 2, 1.0, BLK + 1.0)
    lower = jnp.exp(-place * tq) * fall
    upper = jnp.where(sub < 2, rho_q, 1.0) * rise
    y_hi = jnp.where(positive, (upper - end_q * lower) * inv_q, (BLK * first + place * fall) * (1.0 / N))
    y_lo = lower - end_q * y_hi

    def both(value):
        return jnp.concatenate([value[0:2] + value[2:4], jnp.zeros((2, 128), F32)], axis=0)

    x_lo = scale * jnp.exp(-ts) * at_lo
    x_hi = scale * at_hi
    alpha = (end_s * x_hi - x_lo) * inv_s
    beta = (end_s * x_lo - x_hi) * inv_s
    phi_lo = 2.0 * sinh_s * (x_lo + end_s * beta)
    phi_hi = 2.0 * sinh_s * (x_hi + end_s * alpha)
    w_lo = (2.0 - es) * phi_lo - (2.0 - eq) * (both(y_lo) * inv_pq)
    w_hi = (2.0 - es) * phi_hi - (2.0 - eq) * (both(y_hi) * inv_pq)
    wall_lo = jnp.where(sub < 2, (m_same * w_lo - m_cross * w_hi) * inv_det, 0.0) - x_lo
    wall_hi = jnp.where(sub < 2, (m_same * w_hi - m_cross * w_lo) * inv_det, 0.0) - x_hi
    alpha = (wall_lo - end_s * wall_hi) * inv_s
    beta = (wall_hi - end_s * wall_lo) * inv_s

    power = [None, rho]
    for _ in range(GRP - 1):
        power.append(power[-1] * rho)
    for k in range(segments):
        up = scale * from_lo[k] + alpha * jnp.exp((BLK - 1.0 - BLK * GRP * k) * ts)
        down = scale * from_hi[k] + beta * jnp.exp((BLK * GRP * (k + 1.0) - NY) * ts)
        for i in range(GRP):
            d = GRP * k + i
            value = o_ref[d, 0:4, :] + power[i + 1] * up + power[GRP - i] * down
            o_ref[d, 0:4, :] = value
            if d:
                o_ref[d - 1, 4:8, :] = value
    o_ref[CHIPS - 1, 4:8, :] = x_hi + alpha * end_s + beta


def middle_kernel(b_ref, mid_ref, ratio_ref, own_ref, send_ref):
    core, _, _ = position()

    def tiles(lower, upper):
        @pl.loop(0, GRP, unroll=2)
        def _(i):
            ratio = ratio_ref[pl.ds(pl.multiple_of(8 * i, 8), 8), :]
            for c in range(4):
                a = b_ref[pl.ds(64 * i + c, 8, stride=8), :]
                b = b_ref[pl.ds(64 * i + 4 + c, 8, stride=8), :]
                x = ratio * (a + b) + mid_ref[i, c]
                lower[i, c] = a
                lower[i, 4 + c] = x
                upper[i, c] = x
                upper[i, 4 + c] = b

    @pl.when(core == 0)
    def _():
        tiles(own_ref, send_ref)

    @pl.when(core != 0)
    def _():
        tiles(send_ref, own_ref)


def points_kernel(other, x_ref, ends, q_ref, *refs):
    o_ref, buf, sems = refs[-3:]
    core, _, _ = position()
    chunks = sems.shape[0]
    per = GRP // chunks

    def tile(i, lanes):
        rows = pl.ds(pl.multiple_of(8 * i, 8), 8)
        ps = chain(H2 * (q_ref[rows, :] + SHIFT), PTS)
        ratio = [None] + [ps[m] / ps[m + 1] for m in range(1, PTS)]
        for c in range(4):
            a = ends[i, c]
            y = [None, KAPPA * x_ref[1, c, rows, lanes] + a]
            for m in range(2, PTS):
                y.append(KAPPA * x_ref[m, c, rows, lanes] + ratio[m - 1] * y[-1])
            buf[0, c, rows, :] = a
            value = ends[i, 4 + c]
            for m in range(PTS - 1, 0, -1):
                value = ratio[m] * (y[m] + value)
                buf[m, c, rows, :] = value

    def copy(g, half):
        rows = pl.ds(8 * per * g, 8 * per)
        return pltpu.make_async_copy(
            buf.at[:, :, rows, :], o_ref.at[:, :, rows, pl.ds(128 * half, 128)], sems.at[g]
        )

    for half in range(2):
        @pl.when(core == (1 - half if other else half))
        def _():
            for g in range(chunks):
                @pl.loop(per * g, per * (g + 1), unroll=2)
                def _(i):
                    tile(i, slice(128 * half, 128 * half + 128))

                copy(g, half).start()

    for g in range(chunks):
        copy(g, 0).wait()


def in_vmem(value):
    return pltpu.with_memory_space_constraint(value, pltpu.VMEM)


def local_call(kernel, operands, shapes):
    return pl.pallas_call(
        kernel,
        in_specs=[pl.BlockSpec(memory_space=pltpu.VMEM)] * len(operands),
        out_specs=[pl.BlockSpec(memory_space=pltpu.VMEM)] * len(shapes),
        out_shape=[pltpu.VMEM(shape, F32) for shape in shapes],
        compiler_params=pltpu.CompilerParams(vmem_limit_bytes=8 << 20),
    )(*[in_vmem(v) for v in operands])


def on_device(forcing, kx_wave, kz_wave):
    both = ("kx", "kz")
    wave_groups = [
        [32 * (j // 4) + wave_member(j, ty, tx) for j in range(32)] for ty in range(4) for tx in range(2)
    ]
    core_groups = [[2 * k + c for k in range(CHIPS)] for c in range(2)]
    pairs = [(i, i ^ 1) for i in range(32)]

    vmem = pl.BlockSpec(memory_space=pltpu.VMEM)
    hbm = pl.BlockSpec(memory_space=pltpu.HBM)
    params = pltpu.CompilerParams(vmem_limit_bytes=8 << 20)
    half_shape = (PTS, 4, 128, 128)

    swapped = lax.ppermute(forcing, "kz", pairs)

    payload = pl.pallas_call(
        waves_kernel,
        in_specs=[hbm] * 2,
        out_specs=vmem,
        out_shape=pltpu.VMEM((32, 2, 128), F32),
        scratch_shapes=[
            pltpu.SMEM(kx_wave.shape, jnp.int32),
            pltpu.SMEM(kz_wave.shape, jnp.int32),
            pltpu.SemaphoreType.DMA((2,)),
        ],
        compiler_params=params,
    )(*[pltpu.with_memory_space_constraint(v, pltpu.HBM) for v in (kx_wave, kz_wave)])
    waves = lax.all_to_all(payload, both, 0, 0, tiled=True, axis_index_groups=wave_groups)
    turn = lax.ppermute(waves, "kz", [(i, i ^ 2) for i in range(0, 32, 2)])

    up, mid, q_own, q_oth, ratio = pl.pallas_call(
        moments_kernel,
        in_specs=[vmem, hbm, vmem, vmem],
        out_specs=[vmem] * 5,
        out_shape=[
            pltpu.VMEM(shape, F32)
            for shape in ((CHIPS, 3, 4, 128), (GRP, 4, 8, 128), (128, 128), (128, 128), (128, 128))
        ],
        scratch_shapes=[
            pltpu.VMEM(half_shape, F32),
            pltpu.VMEM((NUM * CHIPS, 128), F32),
            pltpu.SemaphoreType.DMA((4,)),
        ],
        compiler_params=params,
    )(in_vmem(waves), pltpu.with_memory_space_constraint(forcing, pltpu.HBM), in_vmem(swapped), in_vmem(turn))
    blocks = lax.all_to_all(up, both, 0, 0, tiled=True, axis_index_groups=core_groups)
    (ends,) = local_call(solve_kernel, (blocks, q_own), ((CHIPS, 8, 128),))
    ends = lax.all_to_all(ends, both, 0, 0, tiled=True, axis_index_groups=core_groups)
    ends = ends.reshape(8 * CHIPS, 128)
    own, send = local_call(middle_kernel, (ends, mid, ratio), ((GRP, 8, 8, 128),) * 2)
    received = lax.ppermute(send, "kz", pairs)

    def points(other, operands, *made):
        return pl.pallas_call(
            functools.partial(points_kernel, other),
            in_specs=[vmem] * 3 + [hbm] * len(made),
            out_specs=hbm,
            out_shape=pltpu.HBM(forcing.shape, F32),
            input_output_aliases={3: 0} if made else {},
            scratch_shapes=[pltpu.VMEM(half_shape, F32), pltpu.SemaphoreType.DMA((4,))],
            compiler_params=params,
            cost_estimate=pl.CostEstimate(flops=8 << 20, bytes_accessed=4 << 20, transcendentals=0),
        )(*[in_vmem(v) for v in operands], *made)

    fields = points(False, (forcing, own, q_own))
    return points(True, (forcing, received, q_oth), fields)


def solution(mesh):
    placed = (P(("kx", "kz"), None, None, None), P("kx"), P("kz"))
    return jax.shard_map(
        on_device,
        mesh=mesh,
        in_specs=placed,
        out_specs=P(("kx", "kz"), None, None, None),
        check_vma=False,
    )
```

```python
import functools

import jax
import jax.numpy as jnp
from jax import lax
from jax.experimental import pallas as pl
from jax.experimental.pallas import tpu as pltpu
from jax.sharding import PartitionSpec as P

NY = 1536
N = NY + 1
H2 = (2.0 / N) ** 2
SHIFT = 4000.0
KAPPA = SHIFT * H2
ALPHA_X = 0.25
BETA_Z = 2.0 / 3.0
PTS = 6
BLK = 12
GRP = 16
CHIPS = 128
NUM = 12
F32 = jnp.float32


def position():
    iz = lax.axis_index("kz")
    return lax.rem(iz, 2), lax.axis_index("kx"), lax.div(iz, 2)


def wave_group():
    ix = lax.axis_index("kx")
    iz = lax.axis_index("kz")
    x_lo, y = lax.div(ix, 4), lax.rem(ix, 4)
    z, x_hi = lax.div(iz, 4), lax.rem(lax.div(iz, 2), 2)
    return lax.rem(y - z + 8, 4), lax.rem(x_lo + x_hi, 2)


def wave_member(j, ty, tx):
    x_lo, y, b, core = j // 16, j // 4 % 4, j // 2 % 2, j % 2
    return 4 * ((y - ty + 4) % 4 + 4 * b) + 2 * ((x_lo + tx) % 2) + core


def chain(eps, n):
    p = [None, jnp.ones_like(eps)]
    diff = 1.0 + eps
    for _ in range(2, n + 1):
        p.append(p[-1] + diff)
        diff = diff + eps * p[-1]
    return p


def angle(eps):
    x2 = 0.25 * eps
    series = 1.0 + x2 * (-1.0 / 6.0 + x2 * (3.0 / 40.0 + x2 * (-15.0 / 336.0 + x2 * (105.0 / 3456.0))))
    return jnp.sqrt(eps) * series


def waves_kernel(kx_hbm, kz_hbm, o_ref, kx_ref, kz_ref, sems):
    copies = [
        pltpu.make_async_copy(kx_hbm, kx_ref, sems.at[0]),
        pltpu.make_async_copy(kz_hbm, kz_ref, sems.at[1]),
    ]
    for copy in copies:
        copy.start()
    for copy in copies:
        copy.wait()
    iz = lax.axis_index("kz")
    part = 2 * lax.div(iz, 16) + lax.rem(iz, 2)
    lane = lax.broadcasted_iota(jnp.int32, (2, 128), 1)
    kx = jnp.zeros((2, 128), jnp.int32)
    kz = jnp.zeros((2, 128), jnp.int32)
    for r in range(4):
        kx = jnp.where(lax.rem(lane, 4) == r, kx_ref[4 * part + r], kx)
    for r in range(8):
        kz = jnp.where(lax.rem(lane, 8) == r, kz_ref[r], kz)
    rows = jnp.where(lax.broadcasted_iota(jnp.int32, (2, 128), 0) == 0, kz, kx).astype(F32)
    for j in range(o_ref.shape[0]):
        o_ref[j] = rows


def moments_kernel(w_ref, x_ref, r_ref, turn_ref, up_ref, mid_ref, q_ref, qo_ref, ratio_ref, x_own, stage, sems):
    core, _, _ = position()
    ty, tx = wave_group()
    chunks = sems.shape[0]
    per = GRP // chunks

    def copy(g, half):
        rows = pl.ds(8 * per * g, 8 * per)
        return pltpu.make_async_copy(
            x_ref.at[:, :, rows, pl.ds(128 * half, 128)], x_own.at[:, :, rows, :], sems.at[g]
        )

    for half in range(2):
        @pl.when(core == half)
        def _():
            for g in range(chunks):
                copy(g, half).start()

    lane = lax.broadcasted_iota(jnp.int32, (8, 128), 1)
    sub = lax.broadcasted_iota(jnp.int32, (8, 128), 0)
    places = [wave_member(j, ty, tx) for j in range(32)]

    def kz_row(half):
        acc = [jnp.zeros((1, 128), F32) for _ in range(4)]
        for j in range(32):
            acc[j % 4] = jnp.where(lane[0:1] // 8 == places[j] - GRP * half, w_ref[j, 0:1, :], acc[j % 4])
        row = (acc[0] + acc[1]) + (acc[2] + acc[3])
        return (BETA_Z * jnp.broadcast_to(row, (8, 128))) ** 2

    def kx_column(i):
        rows = jnp.where(sub < 4, w_ref[2 * i, 1:2, :], w_ref[2 * i + 1, 1:2, :])
        column = jnp.sum(jnp.where(lane == lax.rem(sub, 4), rows, 0.0), axis=1, keepdims=True)
        return (ALPHA_X * jnp.broadcast_to(column, (8, 128))) ** 2

    kz_own = kz_row(core)
    kz_oth = kz_row(1 - core)
    for i in range(GRP):
        kx = kx_column(i)
        q_ref[8 * i : 8 * i + 8, :] = kx + kz_own
        qo_ref[8 * i : 8 * i + 8, :] = kx + kz_oth

    def tiles(g, first, second):
        @pl.loop(per * g, per * (g + 1), unroll=2)
        def _(i):
            rows = pl.ds(pl.multiple_of(8 * i, 8), 8)
            q = q_ref[rows, :]
            ps = chain(H2 * (q + SHIFT), BLK)
            pq = chain(H2 * q, BLK)
            ratio = ps[PTS] / ps[BLK]
            ratio_ref[rows, :] = ratio
            def put(n, value):
                stage[pl.ds(8 * NUM * i + n, 8, stride=NUM), :] = KAPPA * value

            for c in range(4):
                f = [first(m, c, rows) for m in range(PTS)] + [second(m, c, rows) for m in range(PTS)]
                own = ps[BLK] * f[0]
                nxt = jnp.zeros_like(own)
                mid = jnp.zeros_like(own)
                for m in range(1, BLK):
                    to_own = ps[BLK - m] * f[m]
                    to_nxt = ps[m] * f[m]
                    own = own + to_own
                    nxt = nxt + to_nxt
                    mid = mid + (to_nxt if m <= PTS else to_own)
                put(c, own)
                put(4 + c, nxt)
                mid_ref[i, c] = ratio * (KAPPA * mid)
                if c < 2:
                    own = pq[BLK] * f[0]
                    nxt = pq[1] * f[1]
                    for m in range(1, BLK):
                        own = own + pq[BLK - m] * f[m]
                    for m in range(2, BLK):
                        nxt = nxt + pq[m] * f[m]
                    put(8 + c, own)
                    put(10 + c, nxt)

    for g in range(chunks):
        copy(g, 0).wait()

        @pl.when(core == 0)
        def _():
            tiles(g, lambda m, c, rows: x_own[m, c, rows, :], lambda m, c, rows: r_ref[m, c, rows, :128])

        @pl.when(core != 0)
        def _():
            tiles(g, lambda m, c, rows: r_ref[m, c, rows, 128:], lambda m, c, rows: x_own[m, c, rows, :])

    @pl.loop(0, 64, unroll=4)
    def _(i):
        for k in range(3):
            value = stage[pl.ds(pl.multiple_of(24 * i + 8 * k, 8), 8), :]
            for half in range(2):
                j, a = divmod(2 * k + half, 3)
                up_ref[2 * i + j, a] = value[4 * half : 4 * half + 4, :]


def solve_kernel(m_ref, q_ref, o_ref):
    _, group, chip = position()
    shape = (4, 128)
    q = jnp.broadcast_to(q_ref[pl.ds(GRP * group + chip, 1), :], shape)
    sub = lax.broadcasted_iota(jnp.int32, shape, 0)
    es = H2 * (q + SHIFT)
    eq = H2 * q
    ts = angle(es)
    tq = angle(eq)
    rho = jnp.exp(-BLK * ts)
    rho_seg = jnp.exp(-(BLK * GRP) * ts)
    rho_q = jnp.exp(-BLK * tq)
    rho_q_seg = jnp.exp(-(BLK * GRP) * tq)
    sinh_s = jnp.sqrt(es * (1.0 + 0.25 * es))
    sinh_q = jnp.sqrt(eq * (1.0 + 0.25 * eq))
    scale = 0.5 / (sinh_s * chain(es, BLK)[BLK])
    end_s = jnp.exp(-N * ts)
    inv_s = 1.0 / (1.0 - end_s * end_s)
    end_q = jnp.exp(-N * tq)
    positive = q > 0.0
    inv_q = 1.0 / jnp.where(positive, 1.0 - end_q * end_q, 1.0)
    coth_s = sinh_s * (1.0 + end_s * end_s) * inv_s
    csch_s = 2.0 * sinh_s * end_s * inv_s
    coth_q = jnp.where(positive, sinh_q * (1.0 + end_q * end_q) * inv_q, 1.0 / N)
    csch_q = jnp.where(positive, 2.0 * sinh_q * end_q * inv_q, 1.0 / N)
    m_same = (2.0 - es) * coth_s - (2.0 - eq) * coth_q + 0.5 * (es * es - eq * eq)
    m_cross = (2.0 - eq) * csch_q - (2.0 - es) * csch_s
    inv_det = 1.0 / (m_same * m_same - m_cross * m_cross)
    inv_pq = 1.0 / chain(eq, BLK)[BLK]

    segments = CHIPS // GRP
    ends, heads, falls, rises, firsts = [], [], [], [], []
    for k in range(segments):
        t = []
        for d in range(GRP * k, GRP * (k + 1)):
            value = m_ref[d, 0]
            t.append(value + m_ref[d - 1, 1] if d else value)
        ahead = [t[0]]
        for v in t[1:]:
            ahead.append(rho * ahead[-1] + v)
        ends.append(ahead[-1])
        back = t[-1]
        o_ref[GRP * k + GRP - 1, 0:4, :] = scale * ahead[-1]
        for i in range(GRP - 2, -1, -1):
            o_ref[GRP * k + i, 0:4, :] = scale * (ahead[i] + rho * back)
            back = t[i] + rho * back
        heads.append(back)
        w = [m_ref[d, 2] for d in range(GRP * k, GRP * (k + 1))]
        rise = w[0]
        first = (GRP * k) * w[0]
        for i in range(1, GRP):
            rise = rho_q * rise + w[i]
            first = first + (GRP * k + i) * w[i]
        fall = w[-1]
        for i in range(GRP - 2, -1, -1):
            fall = w[i] + rho_q * fall
        falls.append(fall)
        rises.append(rise)
        firsts.append(first)

    last = m_ref[CHIPS - 1, 1]
    from_lo = [jnp.zeros(shape, F32)]
    for k in range(segments):
        from_lo.append(ends[k] + rho_seg * from_lo[-1])
    at_hi = rho * from_lo[segments] + last
    from_hi = [None] * segments
    value = last
    for k in range(segments - 1, -1, -1):
        from_hi[k] = value
        value = heads[k] + rho_seg * value
    at_lo = value
    fall, rise, first = falls[-1], rises[0], firsts[0]
    for k in range(1, segments):
        fall = falls[segments - 1 - k] + rho_q_seg * fall
        rise = rises[k] + rho_q_seg * rise
        first = first + firsts[k]

    place = jnp.where(sub < 2, 1.0, BLK + 1.0)
    lower = jnp.exp(-place * tq) * fall
    upper = jnp.where(sub < 2, rho_q, 1.0) * rise
    y_hi = jnp.where(positive, (upper - end_q * lower) * inv_q, (BLK * first + place * fall) * (1.0 / N))
    y_lo = lower - end_q * y_hi

    def both(value):
        return jnp.concatenate([value[0:2] + value[2:4], jnp.zeros((2, 128), F32)], axis=0)

    x_lo = scale * jnp.exp(-ts) * at_lo
    x_hi = scale * at_hi
    alpha = (end_s * x_hi - x_lo) * inv_s
    beta = (end_s * x_lo - x_hi) * inv_s
    phi_lo = 2.0 * sinh_s * (x_lo + end_s * beta)
    phi_hi = 2.0 * sinh_s * (x_hi + end_s * alpha)
    w_lo = (2.0 - es) * phi_lo - (2.0 - eq) * (both(y_lo) * inv_pq)
    w_hi = (2.0 - es) * phi_hi - (2.0 - eq) * (both(y_hi) * inv_pq)
    wall_lo = jnp.where(sub < 2, (m_same * w_lo - m_cross * w_hi) * inv_det, 0.0) - x_lo
    wall_hi = jnp.where(sub < 2, (m_same * w_hi - m_cross * w_lo) * inv_det, 0.0) - x_hi
    alpha = (wall_lo - end_s * wall_hi) * inv_s
    beta = (wall_hi - end_s * wall_lo) * inv_s

    power = [None, rho]
    for _ in range(GRP - 1):
        power.append(power[-1] * rho)
    for k in range(segments):
        up = scale * from_lo[k] + alpha * jnp.exp((BLK - 1.0 - BLK * GRP * k) * ts)
        down = scale * from_hi[k] + beta * jnp.exp((BLK * GRP * (k + 1.0) - NY) * ts)
        for i in range(GRP):
            d = GRP * k + i
            value = o_ref[d, 0:4, :] + power[i + 1] * up + power[GRP - i] * down
            o_ref[d, 0:4, :] = value
            if d:
                o_ref[d - 1, 4:8, :] = value
    o_ref[CHIPS - 1, 4:8, :] = x_hi + alpha * end_s + beta


def middle_kernel(b_ref, mid_ref, ratio_ref, own_ref, send_ref):
    core, _, _ = position()

    def tiles(lower, upper):
        @pl.loop(0, GRP, unroll=2)
        def _(i):
            ratio = ratio_ref[pl.ds(pl.multiple_of(8 * i, 8), 8), :]
            numbers = jnp.swapaxes(b_ref[pl.ds(pl.multiple_of(8 * i, 8), 8)], 0, 1)
            for c in range(4):
                a = numbers[c]
                b = numbers[4 + c]
                x = ratio * (a + b) + mid_ref[i, c]
                lower[i, c] = a
                lower[i, 4 + c] = x
                upper[i, c] = x
                upper[i, 4 + c] = b

    @pl.when(core == 0)
    def _():
        tiles(own_ref, send_ref)

    @pl.when(core != 0)
    def _():
        tiles(send_ref, own_ref)


def points_kernel(other, x_ref, ends, q_ref, *refs):
    o_ref, buf, sems = refs[-3:]
    core, _, _ = position()
    chunks = sems.shape[0]
    per = GRP // chunks

    def tile(i, lanes):
        rows = pl.ds(pl.multiple_of(8 * i, 8), 8)
        ps = chain(H2 * (q_ref[rows, :] + SHIFT), PTS)
        ratio = [None] + [ps[m] / ps[m + 1] for m in range(1, PTS)]
        for c in range(4):
            a = ends[i, c]
            y = [None, KAPPA * x_ref[1, c, rows, lanes] + a]
            for m in range(2, PTS):
                y.append(KAPPA * x_ref[m, c, rows, lanes] + ratio[m - 1] * y[-1])
            buf[0, c, rows, :] = a
            value = ends[i, 4 + c]
            for m in range(PTS - 1, 0, -1):
                value = ratio[m] * (y[m] + value)
                buf[m, c, rows, :] = value

    def copy(g, half):
        rows = pl.ds(8 * per * g, 8 * per)
        return pltpu.make_async_copy(
            buf.at[:, :, rows, :], o_ref.at[:, :, rows, pl.ds(128 * half, 128)], sems.at[g]
        )

    for half in range(2):
        @pl.when(core == (1 - half if other else half))
        def _():
            for g in range(chunks):
                @pl.loop(per * g, per * (g + 1), unroll=2)
                def _(i):
                    tile(i, slice(128 * half, 128 * half + 128))

                copy(g, half).start()

    for g in range(chunks):
        copy(g, 0).wait()


def in_vmem(value):
    return pltpu.with_memory_space_constraint(value, pltpu.VMEM)


def local_call(kernel, operands, shapes):
    return pl.pallas_call(
        kernel,
        in_specs=[pl.BlockSpec(memory_space=pltpu.VMEM)] * len(operands),
        out_specs=[pl.BlockSpec(memory_space=pltpu.VMEM)] * len(shapes),
        out_shape=[pltpu.VMEM(shape, F32) for shape in shapes],
        compiler_params=pltpu.CompilerParams(vmem_limit_bytes=8 << 20),
    )(*[in_vmem(v) for v in operands])


def on_device(forcing, kx_wave, kz_wave):
    both = ("kx", "kz")
    wave_groups = [
        [32 * (j // 4) + wave_member(j, ty, tx) for j in range(32)] for ty in range(4) for tx in range(2)
    ]
    core_groups = [[2 * k + c for k in range(CHIPS)] for c in range(2)]
    pairs = [(i, i ^ 1) for i in range(32)]

    vmem = pl.BlockSpec(memory_space=pltpu.VMEM)
    hbm = pl.BlockSpec(memory_space=pltpu.HBM)
    params = pltpu.CompilerParams(vmem_limit_bytes=8 << 20)
    half_shape = (PTS, 4, 128, 128)

    swapped = lax.ppermute(forcing, "kz", pairs)

    payload = pl.pallas_call(
        waves_kernel,
        in_specs=[hbm] * 2,
        out_specs=vmem,
        out_shape=pltpu.VMEM((32, 2, 128), F32),
        scratch_shapes=[
            pltpu.SMEM(kx_wave.shape, jnp.int32),
            pltpu.SMEM(kz_wave.shape, jnp.int32),
            pltpu.SemaphoreType.DMA((2,)),
        ],
        compiler_params=params,
    )(*[pltpu.with_memory_space_constraint(v, pltpu.HBM) for v in (kx_wave, kz_wave)])
    waves = lax.all_to_all(payload, both, 0, 0, tiled=True, axis_index_groups=wave_groups)
    turn = lax.ppermute(waves, "kz", [(i, i ^ 2) for i in range(0, 32, 2)])

    up, mid, q_own, q_oth, ratio = pl.pallas_call(
        moments_kernel,
        in_specs=[vmem, hbm, vmem, vmem],
        out_specs=[vmem] * 5,
        out_shape=[
            pltpu.VMEM(shape, F32)
            for shape in ((CHIPS, 3, 4, 128), (GRP, 4, 8, 128), (128, 128), (128, 128), (128, 128))
        ],
        scratch_shapes=[
            pltpu.VMEM(half_shape, F32),
            pltpu.VMEM((NUM * (CHIPS + 8), 128), F32),
            pltpu.SemaphoreType.DMA((4,)),
        ],
        compiler_params=params,
    )(in_vmem(waves), pltpu.with_memory_space_constraint(forcing, pltpu.HBM), in_vmem(swapped), in_vmem(turn))
    blocks = lax.all_to_all(up, both, 0, 0, tiled=True, axis_index_groups=core_groups)
    (ends,) = local_call(solve_kernel, (blocks, q_own), ((CHIPS, 8, 128),))
    ends = lax.all_to_all(ends, both, 0, 0, tiled=True, axis_index_groups=core_groups)
    own, send = local_call(middle_kernel, (ends, mid, ratio), ((GRP, 8, 8, 128),) * 2)
    received = lax.ppermute(send, "kz", pairs)

    def points(other, operands, *made):
        return pl.pallas_call(
            functools.partial(points_kernel, other),
            in_specs=[vmem] * 3 + [hbm] * len(made),
            out_specs=hbm,
            out_shape=pltpu.HBM(forcing.shape, F32),
            input_output_aliases={3: 0} if made else {},
            scratch_shapes=[pltpu.VMEM(half_shape, F32), pltpu.SemaphoreType.DMA((4,))],
            compiler_params=params,
            cost_estimate=pl.CostEstimate(flops=8 << 20, bytes_accessed=4 << 20, transcendentals=0),
        )(*[in_vmem(v) for v in operands], *made)

    fields = points(False, (forcing, own, q_own))
    return points(True, (forcing, received, q_oth), fields)


def solution(mesh):
    placed = (P(("kx", "kz"), None, None, None), P("kx"), P("kz"))
    return jax.shard_map(
        on_device,
        mesh=mesh,
        in_specs=placed,
        out_specs=P(("kx", "kz"), None, None, None),
        check_vma=False,
    )
```
